1024 devices in a mesh: tm: 32 (over z, core), expert: 16 (over x_lo, y), dp: 2 (over x_hi).
Axes of the slice: x: 4 (x_hi: 2, x_lo: 2; x = x_hi * 2 + x_lo), y: 8, z: 16, core: 2. Of those that a mesh axis runs over, the one named last changes fastest.
Arguments:
- resid: bfloat16 [2, 4096, 1024], P('dp', 'tm'), may hold values from -6 to 6
- glu_input: bfloat16 [2, 4096, 2048], P('dp', 'tm'), may hold values from -8 to 8
- dw_kernel: float32 [31, 1024], replicated, may hold values from -2 to 2
- w_in: bfloat16 [32, 1024, 4096], P('tm', None, 'expert'), may hold values from -0.1875 to 0.1875
- w_out: bfloat16 [32, 4096, 1024], P('tm', 'expert'), may hold values from -0.1875 to 0.1875
- expert_ids: int32 [2, 4096, 2], P('dp', 'tm'), may hold values from 0 to 31, all different within a row; in each aligned block of 128 rows (0 to 127, 128 to 255, ..., all dimensions but the last counted through in order) at most 16 rows name the same one
- mix_weights: float32 [2, 4096, 2], P('dp', 'tm'), may hold values from 0.2 to 1
- frame_kept: int32 [2, 4096], P('dp', 'tm'), may hold values 0 or 1
- out_grad: bfloat16 [2, 4096, 1024], P('dp', 'tm'), may hold values from -6 to 6
Outputs:
- block_out: bfloat16 [2, 4096, 1024], P('dp', 'tm')
- resid_grad: bfloat16 [2, 4096, 1024], P('dp', 'tm')
- glu_grad: bfloat16 [2, 4096, 2048], P('dp', 'tm')
- w_in_grad: float32 [32, 1024, 4096], P('tm', 'dp', 'expert')
- w_out_grad: float32 [32, 4096, 1024], P('tm', 'expert', 'dp')
The draws below stay inside these ranges and needn't reach their ends.
Inputs may be any that keep to these rules, and one draw needn't show every extreme that they name: `expert_ids`: the two ids of a frame differ. Among the rows of one device (aligned blocks of 128 frames) no expert is named more than 16 times, a bound that some block reaches.
All inputs are finite; a program needn't handle non-finite values. No bound on the sum of `frame_kept` on one device may be relied on, other than what follows from the above.
Results may differ from the reference program's by a relative error of at most 0.023.
Values may be sent and summed in bfloat16 or wider, within the bound.
No kernel may reach another device: no remote copies, remote signals or barrier semaphores. Data moves between devices by JAX's collectives and lax.ppermute only.
A program may use at most 128 MiB of HBM per device.

```python
import math
import jax
import jax.numpy as jnp
import numpy as np
from jax import lax

D = 1024
H = 4096
KERNEL = 31
FR_DEV = 128
EXPERTS = 32
CAP = 16
FRAMES = 4096
UTT = 2
N_EXPERT = 16


def place_ends(values, key, least, largest):
    longest = values.shape.index(max(values.shape))
    spots = []
    for shift in (0, 1):
        where = [jax.random.randint(jax.random.fold_in(key, axis), (), 0, length) for axis, length in enumerate(values.shape)]
        where[longest] = (where[longest] + shift) % values.shape[longest]
        spots.append(tuple(where))
    return values.at[spots[0]].set(least).at[spots[1]].set(largest)


def block_scale(rng, dims, pieces, low, largest):
    gain = 1.0
    for axis_at, blocks in pieces:
        steps = jax.random.uniform(jax.random.fold_in(jax.random.fold_in(rng, 6), axis_at), (blocks,), jnp.float32, low / len(pieces), largest / len(pieces))
        gain = gain * jnp.repeat(jnp.exp(steps), dims[axis_at] // blocks).reshape((-1,) + (1,) * (len(dims) - 1 - axis_at))
    return gain


def routed_block(own_key, own, number, rows, count, top, most, lean):
    order = jax.random.permutation(own_key, count)
    packed, usual = shares(count, rows * top, most, lean, True), shares(count, rows * top, most, lean, False)
    places = jnp.arange(count)

    def named(sizes, rotation):
        used = int((sizes > 0).sum())
        fixed = max(1, used // 4)
        shifted = fixed + (places - fixed + rotation * (used - fixed)) % max(1, count - fixed)
        return jnp.zeros((count,), jnp.int32).at[order[jnp.where(places < fixed, places, shifted)]].set(jnp.asarray(sizes, jnp.int32))

    sizes = jnp.where(number % 4 == 0, named(packed, number // 4), named(usual, number - number // 4 - 1))
    mixed = jax.random.permutation(jax.random.fold_in(own, 3), count)
    donor, taker = mixed[0:count // 2 * 2:2], mixed[1:count // 2 * 2:2]
    margin = jnp.minimum(sizes[donor] - 1, most - sizes[taker]) // 2
    margin = jnp.where((donor == order[0]) | (taker == order[0]) | (sizes[taker] == 0), 0, jnp.maximum(margin, 0))
    shifted = jax.random.randint(jax.random.fold_in(own, 4), (count // 2,), 0, 1 << 20) % (margin + 1)
    sizes = sizes.at[donor].add(-shifted).at[taker].add(shifted)
    members = jnp.searchsorted(jnp.cumsum(sizes), jnp.arange(rows * top), side="right").astype(jnp.int32)
    grid = members.reshape(top, rows).T
    grid = grid[jax.random.permutation(jax.random.fold_in(own, 1), rows)]
    rotation = jax.random.randint(jax.random.fold_in(own, 2), (rows, 1), 0, top)
    return jnp.take_along_axis(grid, (jnp.arange(top)[None, :] + rotation) % top, axis=1)


def shares(count, total, most, lean, full):
    portions = [(1 << 20) // math.isqrt(rank ** lean) + 1 for rank in range(1, count + 1)]
    largest = most if full else min(most, max(-(-total // count), total * portions[0] // sum(portions)))
    least = 1 if total - largest >= count - 1 else 0
    counts, spare = [largest] + [least] * (count - 1), total - largest - least * (count - 1)
    while spare > 0:
        free = [i for i in range(1, count) if counts[i] < largest] or [i for i in range(1, count) if counts[i] < most]
        pool, left = sum([portions[i] for i in free]), spare
        for i in free:
            more = min(most - counts[i], max(1, left * portions[i] // pool), spare)
            counts[i] = counts[i] + more
            spare = spare - more
    return np.array(counts)


def gaussian(key, shape, spread, bound, cuts=(), kind=jnp.bfloat16):
    result = spread * jax.random.normal(key, shape, jnp.float32)
    if cuts:
        result = result * block_scale(key, shape, cuts, -0.22, 0.18)
    return jnp.clip(result, -bound, bound).astype(kind)


def setup_inputs(seed: int = 0) -> dict:
    splits = jax.random.split(jax.random.key(seed), 10)
    resid = gaussian(splits[0], (UTT, FRAMES, D), 1.0, 6.0, ((0, 2), (1, 32)))
    glu_input = gaussian(splits[1], (UTT, FRAMES, 2 * D), 1.5, 8.0, ((0, 2), (1, 32)))
    dw_kernel = gaussian(splits[2], (KERNEL, D), (KERNEL // 4) ** -0.5, 2.0, (), jnp.float32)
    w_in = gaussian(splits[3], (EXPERTS, D, H), D ** -0.5, 0.1875, ((0, 32), (2, 16)))
    w_out = gaussian(splits[4], (EXPERTS, H, D), (H // 4) ** -0.5, 0.1875, ((0, 32), (1, 16)))
    expert_ids_keys = jax.random.split(jax.random.fold_in(splits[5], 1), UTT * FRAMES // FR_DEV)
    expert_ids_turns = jax.random.permutation(jax.random.fold_in(splits[5], 3), UTT * FRAMES // FR_DEV)
    expert_ids = jax.vmap(lambda own, number: routed_block(jax.random.fold_in(splits[5], 2), own, number, FR_DEV, EXPERTS, 2, CAP, 2))(expert_ids_keys, expert_ids_turns).reshape((UTT, FRAMES, 2))
    mix_weights = jnp.clip(0.2 + 0.8 * jax.random.uniform(splits[6], (UTT, FRAMES, 2), jnp.float32) ** block_scale(splits[6], (UTT, FRAMES, 2), ((0, 2), (1, 32)), -0.2, 0.2), 0.2, 1.0)
    frame_kept = place_ends((jax.random.randint(splits[7], (UTT, FRAMES), 0, 8) < 7).astype(jnp.int32), jax.random.fold_in(splits[7], 1), 0, 1)
    out_grad = gaussian(splits[8], (UTT, FRAMES, D), 1.0, 6.0, ((0, 2), (1, 32)))
    return {"resid": resid, "glu_input": glu_input, "dw_kernel": dw_kernel, "w_in": w_in, "w_out": w_out, "expert_ids": expert_ids, "mix_weights": mix_weights, "frame_kept": frame_kept, "out_grad": out_grad}


def swish_slope(value):
    sig = jax.nn.sigmoid(value)
    return sig * (1.0 + value * (1.0 - sig))


def reference(resid, glu_input, dw_kernel, w_in, w_out, expert_ids, mix_weights, frame_kept, out_grad):
    half = KERNEL // 2
    value = glu_input[..., :D].astype(jnp.float32)
    gate = glu_input[..., D:].astype(jnp.float32)
    sig_gate = jax.nn.sigmoid(gate)
    glu = value * sig_gate
    padded = jnp.pad(glu, ((0, 0), (half, half), (0, 0)))
    conv = jnp.zeros_like(glu)
    for tap in range(KERNEL):
        conv = conv + dw_kernel[tap][None, None, :] * padded[:, tap:tap + FRAMES, :]
    hidden_in = (resid.astype(jnp.float32) + conv * jax.nn.sigmoid(conv)).astype(jnp.bfloat16)

    blocks = UTT * FRAMES // FR_DEV
    ids = expert_ids.reshape(blocks, 2 * FR_DEV).astype(jnp.int32)
    onehot = (ids[:, :, None] == jnp.arange(EXPERTS, dtype=jnp.int32)[None, None, :]).astype(jnp.int32)
    slot = jnp.sum((jnp.cumsum(onehot, axis=1) - onehot) * onehot, axis=2).astype(jnp.int32)
    block_index = jnp.arange(blocks, dtype=jnp.int32)[:, None]
    rows = blocks * CAP
    dest = (ids * rows + block_index * CAP + slot).reshape(-1).astype(jnp.int32)

    flat_hidden = jnp.repeat(hidden_in.reshape(-1, D), 2, axis=0)
    scale = (mix_weights * frame_kept[..., None].astype(jnp.float32)).reshape(-1)
    flat_grad = out_grad.astype(jnp.float32).reshape(-1, D)
    scaled = (jnp.repeat(flat_grad, 2, axis=0) * scale[:, None]).astype(jnp.bfloat16)
    in_buf = jnp.zeros((EXPERTS * rows, D), jnp.bfloat16).at[dest].set(flat_hidden).reshape(EXPERTS, rows, D)
    grad_buf = jnp.zeros((EXPERTS * rows, D), jnp.bfloat16).at[dest].set(scaled).reshape(EXPERTS, rows, D)
    shard_width = H // N_EXPERT

    def per_expert(items):
        inputs, grads, weight_in, weight_out = items
        pre = jnp.dot(inputs, weight_in, preferred_element_type=jnp.float32)
        act = (pre * jax.nn.sigmoid(pre)).astype(jnp.bfloat16)
        act_blocks = act.reshape(rows, N_EXPERT, shard_width).astype(jnp.float32)
        out_blocks = weight_out.reshape(N_EXPERT, shard_width, D).astype(jnp.float32)
        parts = jnp.einsum('rnh,nhd->nrd', act_blocks, out_blocks).astype(jnp.bfloat16).astype(jnp.float32)
        expert_out = jnp.sum(parts, axis=0)
        back = jnp.dot(grads, weight_out.T, preferred_element_type=jnp.float32)
        act_grad = (back * swish_slope(pre)).astype(jnp.bfloat16)
        grad_blocks = act_grad.reshape(rows, N_EXPERT, shard_width).astype(jnp.float32)
        in_blocks = weight_in.T.reshape(N_EXPERT, shard_width, D).astype(jnp.float32)
        dparts = jnp.einsum('rnh,nhd->nrd', grad_blocks, in_blocks).astype(jnp.bfloat16).astype(jnp.float32)
        input_part = jnp.sum(dparts, axis=0)
        grad_in = jnp.dot(inputs.T, act_grad, preferred_element_type=jnp.float32)
        grad_out = jnp.dot(act.T, grads, preferred_element_type=jnp.float32)
        return expert_out, input_part, grad_in, grad_out

    expert_out, input_part, w_in_grad, w_out_grad = lax.map(per_expert, (in_buf, grad_buf, w_in, w_out))
    picked = expert_out.reshape(-1, D)[dest] * scale[:, None]
    moe = jnp.sum(picked.reshape(UTT * FRAMES, 2, D), axis=1).reshape(UTT, FRAMES, D)
    block_out = (hidden_in.astype(jnp.float32) + moe).astype(jnp.bfloat16)

    taken = input_part.reshape(-1, D)[dest]
    moe_grad = jnp.sum(taken.reshape(UTT * FRAMES, 2, D), axis=1).reshape(UTT, FRAMES, D)
    hid_grad = out_grad.astype(jnp.float32) + moe_grad
    conv_grad = hid_grad * swish_slope(conv)
    padded_grad = jnp.pad(conv_grad, ((0, 0), (half, half), (0, 0)))
    glu_back = jnp.zeros_like(conv_grad)
    for tap in range(KERNEL):
        start = 2 * half - tap
        glu_back = glu_back + dw_kernel[tap][None, None, :] * padded_grad[:, start:start + FRAMES, :]
    glu_grad = jnp.concatenate([glu_back * sig_gate, glu_back * value * sig_gate * (1.0 - sig_gate)], axis=2).astype(jnp.bfloat16)
    return block_out, hid_grad.astype(jnp.bfloat16), glu_grad, w_in_grad, w_out_grad
```

```python
import jax
import jax.numpy as jnp
from jax import lax
from jax.experimental import pallas as pl
from jax.experimental.pallas import tpu as pltpu
from jax.sharding import Mesh, PartitionSpec as P

KERNEL = 31
HALF = KERNEL // 2
F32 = jnp.float32
BF16 = jnp.bfloat16
NT = (((1,), (1,)), ((), ()))
TN = (((0,), (0,)), ((), ()))


def swish_slope(value):
    sig = jax.nn.sigmoid(value)
    return sig * (1.0 + value * (1.0 - sig))


def rims(shard):
    size, length = lax.axis_size("tm"), shard.shape[0]
    up = [(i, i + 1) for i in range(size - 1)]
    down = [(j, i) for i, j in up]
    before = lax.ppermute(shard[length - HALF :], "tm", up)
    after = lax.ppermute(shard[:HALF], "tm", down)
    return before, after


def gather_columns(rows_ref, hid, grad):
    parts = rows_ref.shape[0]
    cols = rows_ref.shape[2] // 2
    for part in range(parts):
        side, at = divmod(part, parts // 2)
        block = rows_ref[part]
        hid[side, :, at * cols : (at + 1) * cols] = block[:, :cols]
        grad[side, :, at * cols : (at + 1) * cols] = block[:, cols:]


def expert_kernel(rows_ref, win_a, win_b, wout_a, wout_b, act_ref, act_grad_ref, out_ref, hid, grad):
    gather_columns(rows_ref, hid, grad)
    width = hid.shape[2]
    result = [0.0, 0.0]
    part = [0.0, 0.0]
    for which, (w_in, w_out) in enumerate(((win_a, wout_a), (win_b, wout_b))):
        pre = sum(
            jnp.dot(hid[s], w_in[s * width : (s + 1) * width, :], preferred_element_type=F32)
            for s in range(2)
        )
        back = sum(
            lax.dot_general(
                grad[s], w_out[:, s * width : (s + 1) * width], NT, preferred_element_type=F32
            )
            for s in range(2)
        )
        sig = jax.nn.sigmoid(pre)
        act = (pre * sig).astype(BF16)
        act_grad = (back * (sig * (1.0 + pre * (1.0 - sig)))).astype(BF16)
        act_ref[which] = act
        act_grad_ref[which] = act_grad
        for s in range(2):
            result[s] += jnp.dot(
                act, w_out[:, s * width : (s + 1) * width], preferred_element_type=F32
            )
            part[s] += lax.dot_general(
                act_grad, w_in[s * width : (s + 1) * width, :], NT, preferred_element_type=F32
            )
    blocks = out_ref.shape[0] // 2
    cols = out_ref.shape[2]
    for index in range(blocks):
        side, at = divmod(index, blocks // 2)
        out_ref[index] = result[side][:, at * cols : (at + 1) * cols].astype(BF16)
        out_ref[blocks + index] = part[side][:, at * cols : (at + 1) * cols].astype(BF16)


def grads_kernel(dp_ref, rows_ref, act_ref, act_grad_ref, own_in, own_out, send, hid, grad):
    gather_columns(rows_ref, hid, grad)
    mine = dp_ref[0]
    hidden = act_ref.shape[2]
    slot = 0
    for which in range(2):
        for other in range(2):
            side = mine if other == 0 else 1 - mine
            g_in = lax.dot_general(hid[side], act_grad_ref[which], TN, preferred_element_type=F32)
            g_out = lax.dot_general(act_ref[which], grad[side], TN, preferred_element_type=F32)
            if which == 0 and other == 0:
                own_in[...] = g_in
                own_out[...] = g_out
            else:
                width = g_in.shape[0]
                send[slot, :width] = g_in.astype(BF16)
                for piece in range(g_out.shape[1] // hidden):
                    send[slot, width + piece * hidden : width + (piece + 1) * hidden] = g_out[
                        :, piece * hidden : (piece + 1) * hidden
                    ].astype(BF16)
                slot += 1


def vmem(count):
    return [pl.BlockSpec(memory_space=pltpu.VMEM)] * count


def expert_rows(rows, win, win_other, wout, wout_other):
    parts, count, pair = rows.shape
    width = parts * pair // 2
    hidden = win.shape[1]
    flops = 16 * count * width * hidden
    return pl.pallas_call(
        expert_kernel,
        out_shape=(
            jax.ShapeDtypeStruct((2, count, hidden), BF16),
            jax.ShapeDtypeStruct((2, count, hidden), BF16),
            jax.ShapeDtypeStruct((2 * parts, count, pair // 2), BF16),
        ),
        in_specs=vmem(5),
        out_specs=tuple(vmem(3)),
        scratch_shapes=[pltpu.VMEM((2, count, width // 2), BF16)] * 2,
        compiler_params=pltpu.CompilerParams(vmem_limit_bytes=40 * 2**20),
        cost_estimate=pl.CostEstimate(flops=flops, bytes_accessed=5 * 2**20, transcendentals=0),
    )(rows, win, win_other, wout, wout_other)


def weight_grads(dp, rows, act, act_grad):
    parts, count, pair = rows.shape
    width = parts * pair // 2
    hidden = act.shape[2]
    return pl.pallas_call(
        grads_kernel,
        out_shape=(
            jax.ShapeDtypeStruct((width // 2, hidden), F32),
            jax.ShapeDtypeStruct((hidden, width // 2), F32),
            jax.ShapeDtypeStruct((3, width, hidden), BF16),
        ),
        in_specs=[pl.BlockSpec(memory_space=pltpu.SMEM)] + vmem(3),
        out_specs=tuple(vmem(3)),
        scratch_shapes=[pltpu.VMEM((2, count, width // 2), BF16)] * 2,
        compiler_params=pltpu.CompilerParams(vmem_limit_bytes=40 * 2**20),
        cost_estimate=pl.CostEstimate(
            flops=8 * count * width * hidden, bytes_accessed=5 * 2**20, transcendentals=0
        ),
    )(dp, rows, act, act_grad)


def shards(resid, glu_input, dw_kernel, w_in, w_out, expert_ids, mix_weights, frame_kept, out_grad):
    frames = resid.shape[1]
    width = resid.shape[2]
    experts = lax.axis_size("tm")
    ranks = lax.axis_size("y")
    capacity = 4 * frames // experts
    half_cap = capacity // 2
    cols = width // ranks
    xl = lax.axis_index("xl")
    y = lax.axis_index("y")
    dp = lax.axis_index("dp")
    weight_in = w_in[0]
    weight_out = w_out[0]
    swap_xl = [(0, 1), (1, 0)]

    glu_in = glu_input[0]
    before, after = rims(glu_in)
    win_other = lax.ppermute(weight_in, "xl", swap_xl)
    wout_other = lax.ppermute(weight_out, "xl", swap_xl)

    ids = expert_ids[0].T.reshape(-1)
    order = 2 * (jnp.arange(2 * frames) % frames) + jnp.arange(2 * frames) // frames
    earlier = (ids[:, None] == ids[None, :]) & (order[None, :] < order[:, None])
    slot = jnp.sum(earlier.astype(jnp.int32), axis=1)
    dest = ids * capacity + slot
    scale = (mix_weights[0] * frame_kept[0][:, None].astype(F32)).T.reshape(-1)
    near = jnp.where(slot // half_cap == xl, ids * half_cap + slot % half_cap, -1)
    near_hot = near[None, :] == jnp.arange(experts * half_cap)[:, None]
    near_frames = (near_hot[:, :frames] | near_hot[:, frames:]).astype(BF16)
    near_scale = jnp.sum(jnp.where(near_hot, scale[None, :], 0.0), axis=1)
    pick = (dest[:, None] == jnp.arange(experts * capacity)[None, :]).astype(BF16)
    pick_scale = jnp.where(xl == 0, scale, 1.0)

    value = glu_in[:, :width].astype(F32)
    gate = glu_in[:, width:].astype(F32)
    sig_gate = jax.nn.sigmoid(gate)
    wide = jnp.concatenate([before, glu_in, after], axis=0).astype(F32)
    padded = wide[:, :width] * jax.nn.sigmoid(wide[:, width:])
    conv = jnp.zeros((frames, width), F32)
    for tap in range(KERNEL):
        conv = conv + dw_kernel[tap][None, :] * padded[tap : tap + frames]
    hidden_in = (resid[0].astype(F32) + conv * jax.nn.sigmoid(conv)).astype(BF16)

    hid_cols = lax.dynamic_slice_in_dim(hidden_in, y * cols, cols, axis=1)
    grad_cols = lax.dynamic_slice_in_dim(out_grad[0], y * cols, cols, axis=1)
    both = jnp.concatenate([hid_cols, grad_cols], axis=1)
    rows = jnp.dot(near_frames, both, preferred_element_type=F32)
    factor = jnp.where(jnp.arange(2 * cols)[None, :] < cols, 1.0, near_scale[:, None])
    rows = (rows * factor).astype(BF16).reshape(experts, half_cap, 2 * cols)
    rows = lax.all_to_all(rows, "tm", 0, 0, tiled=True)
    rows = rows.reshape(1, experts * half_cap, 2 * cols)
    rows = lax.all_to_all(
        jnp.broadcast_to(rows, (ranks,) + rows.shape[1:]), "y", 0, 0, tiled=True
    )

    act, act_grad, parts = expert_rows(rows, weight_in, win_other, weight_out, wout_other)
    parts = lax.all_to_all(parts, ("xl", "y"), 0, 0, tiled=True)
    own_in, own_out, send = weight_grads(dp.reshape(1), rows, act, act_grad)
    got = (
        lax.ppermute(send[0], "dp", swap_xl),
        lax.ppermute(send[1], "xl", swap_xl),
        lax.ppermute(send[2], ("xl", "dp"), [(0, 3), (3, 0), (1, 2), (2, 1)]),
    )

    parts = parts.reshape(2, ranks, experts, half_cap, cols).astype(F32).sum(axis=1)
    parts = parts.astype(BF16).transpose(1, 0, 2, 3).reshape(experts, capacity, cols)
    parts = lax.all_to_all(parts, "tm", 0, 0, tiled=True).reshape(experts * capacity, cols)
    picked = jnp.dot(pick, parts, preferred_element_type=F32) * pick_scale[:, None]
    summed = (picked[:frames] + picked[frames:]).astype(BF16)
    summed = lax.all_to_all(
        jnp.broadcast_to(summed[None], (2 * ranks,) + summed.shape), ("xl", "y"), 0, 0, tiled=True
    )
    moe = summed[:ranks].transpose(1, 0, 2).reshape(frames, width).astype(F32)
    moe_grad = summed[ranks:].transpose(1, 0, 2).reshape(frames, width).astype(F32)
    block_out = (hidden_in.astype(F32) + moe).astype(BF16)
    hid_grad = out_grad[0].astype(F32) + moe_grad

    conv_grad = hid_grad * swish_slope(conv)
    before, after = rims(conv_grad.astype(BF16))
    padded_grad = jnp.concatenate([before.astype(F32), conv_grad, after.astype(F32)], axis=0)
    glu_back = jnp.zeros_like(conv_grad)
    for tap in range(KERNEL):
        start = 2 * HALF - tap
        glu_back = glu_back + dw_kernel[tap][None, :] * padded_grad[start : start + frames]
    glu_grad = jnp.concatenate(
        [glu_back * sig_gate, glu_back * value * sig_gate * (1.0 - sig_gate)], axis=1
    ).astype(BF16)

    hidden = weight_in.shape[1]
    w_in_grad = own_in + sum(piece[: width // 2].astype(F32) for piece in got)
    rest = [
        piece[width // 2 :].reshape(-1, hidden, hidden).transpose(1, 0, 2).reshape(hidden, -1)
        for piece in got
    ]
    w_out_grad = own_out + sum(piece.astype(F32) for piece in rest)
    return (
        block_out[None],
        hid_grad.astype(BF16)[None],
        glu_grad[None],
        w_in_grad[None],
        w_out_grad[None],
    )


def solution(mesh):
    size = mesh.shape["expert"]
    axes = {"tm": mesh.shape["tm"], "xl": 2, "y": size // 2, "dp": mesh.shape["dp"]}
    split = Mesh(mesh.devices.reshape(tuple(axes.values())), tuple(axes))
    expert = ("xl", "y")
    return jax.shard_map(
        shards,
        mesh=split,
        in_specs=(
            P("dp", "tm", None),
            P("dp", "tm", None),
            P(),
            P("tm", None, expert),
            P("tm", expert, None),
            P("dp", "tm", None),
            P("dp", "tm", None),
            P("dp", "tm"),
            P("dp", "tm", None),
        ),
        out_specs=(
            P("dp", "tm", None),
            P("dp", "tm", None),
            P("dp", "tm", None),
            P("tm", "dp", expert),
            P("tm", expert, "dp"),
        ),
        check_vma=False,
    )
```

```python
import jax
import jax.numpy as jnp
from jax import lax
from jax.experimental import pallas as pl
from jax.experimental.pallas import tpu as pltpu
from jax.sharding import Mesh, PartitionSpec as P

KERNEL = 31
HALF = KERNEL // 2
F32 = jnp.float32
BF16 = jnp.bfloat16
NT = (((1,), (1,)), ((), ()))
TN = (((0,), (0,)), ((), ()))


RIM = 16


def swish_slope(value):
    sig = jax.nn.sigmoid(value)
    return sig * (1.0 + value * (1.0 - sig))


def rims(top, bottom):
    size = lax.axis_size("tm")
    up = [(i, i + 1) for i in range(size - 1)]
    down = [(j, i) for i, j in up]
    return lax.ppermute(bottom, "tm", up), lax.ppermute(top, "tm", down)


def taps_sum(padded, taps, frames, start, step):
    total = None
    for residue in range(8):
        offsets = [(start + step * j, j) for j in range(KERNEL) if (start + step * j) % 8 == residue]
        reach = max(offset for offset, _ in offsets) - residue
        shifted = padded[residue : residue + reach + frames, :]
        for offset, j in offsets:
            base = offset - residue
            term = taps[j : j + 1, :] * shifted[base : base + frames]
            total = term if total is None else total + term
    return total


def glu(value, gate):
    return value.astype(F32) * jax.nn.sigmoid(gate.astype(F32))


def glu_conv(value, gate, before_value, before_gate, after_value, after_gate, taps, padded):
    frames = value.shape[0]
    padded[:RIM] = glu(before_value[...], before_gate[...])
    padded[RIM : RIM + frames] = glu(value[...], gate[...])
    padded[RIM + frames :] = glu(after_value[...], after_gate[...])
    return taps_sum(padded, taps, frames, RIM - HALF, 1)


def dispatch_kernel(
    where_ref,
    value,
    gate,
    before_value,
    before_gate,
    after_value,
    after_gate,
    taps,
    resid,
    out_grad,
    dest,
    scale,
    rows_ref,
    padded,
):
    frames = value.shape[0]
    conv = glu_conv(value, gate, before_value, before_gate, after_value, after_gate, taps, padded)
    hidden_in = (resid[...].astype(F32) + conv * jax.nn.sigmoid(conv)).astype(BF16)
    first = where_ref[0] == 0
    chosen = jnp.where(first, hidden_in.astype(F32), out_grad[...].astype(F32)).astype(BF16)
    total = rows_ref.shape[0]
    hot = dest[...] == lax.broadcasted_iota(jnp.int32, (total, 2 * frames), 0)
    factor = jnp.sum(jnp.where(hot, scale[...], 0.0), axis=1, keepdims=True)
    ones = jnp.where(hot, 1.0, 0.0)
    ones = (ones[:, :frames] + ones[:, frames:]).astype(BF16)
    rows = jnp.dot(ones, chosen, preferred_element_type=F32)
    rows_ref[...] = jnp.where(first, rows, rows * factor).astype(BF16)


def forward_kernel(
    value,
    gate,
    before_value,
    before_gate,
    after_value,
    after_gate,
    taps,
    resid,
    hidden_ref,
    slope_ref,
    padded,
):
    conv = glu_conv(value, gate, before_value, before_gate, after_value, after_gate, taps, padded)
    sig = jax.nn.sigmoid(conv)
    hidden_ref[...] = (resid[...].astype(F32) + conv * sig).astype(BF16)
    slope_ref[...] = sig * (1.0 + conv * (1.0 - sig))


def edges_kernel(part_ref, out_grad, slope, edges_ref):
    for at in range(part_ref.shape[0]):
        cols = slice(at * part_ref.shape[2], (at + 1) * part_ref.shape[2])
        hid_grad = out_grad[:, cols].astype(F32) + part_ref[at].astype(F32)
        edges_ref[:, cols] = (hid_grad * slope[:, cols]).astype(BF16)


def outputs_kernel(moe_ref, part_ref, hidden, out_grad, slope, block_ref, resid_ref, conv_grad_ref):
    block_ref[...] = (hidden[...].astype(F32) + moe_ref[0].astype(F32)).astype(BF16)
    hid_grad = out_grad[...].astype(F32) + part_ref[0].astype(F32)
    resid_ref[...] = hid_grad.astype(BF16)
    conv_grad_ref[...] = hid_grad * slope[...]


def backward_kernel(conv_grad, before, after, taps, glu_in, out, padded):
    frames, width = conv_grad.shape
    cols = padded.shape[1]

    def step(index, carry):
        at = pl.ds(pl.multiple_of(index * cols, cols), cols)
        at_gate = pl.ds(pl.multiple_of(width + index * cols, cols), cols)
        padded[:RIM] = before[:, at].astype(F32)
        padded[RIM : RIM + frames] = conv_grad[:, at]
        padded[RIM + frames :] = after[:, at].astype(F32)
        back = taps_sum(padded, taps[:, at], frames, RIM + HALF, -1)
        sig = jax.nn.sigmoid(glu_in[:, at_gate].astype(F32))
        grad = back * sig
        out[:, at] = grad.astype(BF16)
        out[:, at_gate] = (grad * glu_in[:, at].astype(F32) * (1.0 - sig)).astype(BF16)
        return carry

    lax.fori_loop(0, width // cols, step, 0)


def gather_columns(rows_ref, hid, grad):
    parts = rows_ref.shape[0] // 2
    cols = rows_ref.shape[2]
    for part in range(parts):
        side, at = divmod(part, parts // 2)
        hid[side, :, at * cols : (at + 1) * cols] = rows_ref[part]
        grad[side, :, at * cols : (at + 1) * cols] = rows_ref[parts + part]


def expert_kernel(rows_ref, win_a, win_b, wout_a, wout_b, act_ref, act_grad_ref, out_ref, hid, grad):
    gather_columns(rows_ref, hid, grad)
    width = hid.shape[2]
    result = [0.0, 0.0]
    part = [0.0, 0.0]
    for which, (w_in, w_out) in enumerate(((win_a, wout_a), (win_b, wout_b))):
        pre = sum(
            jnp.dot(hid[s], w_in[s * width : (s + 1) * width, :], preferred_element_type=F32)
            for s in range(2)
        )
        back = sum(
            lax.dot_general(
                grad[s], w_out[:, s * width : (s + 1) * width], NT, preferred_element_type=F32
            )
            for s in range(2)
        )
        sig = jax.nn.sigmoid(pre)
        act = (pre * sig).astype(BF16)
        act_grad = (back * (sig * (1.0 + pre * (1.0 - sig)))).astype(BF16)
        act_ref[which] = act
        act_grad_ref[which] = act_grad
        for s in range(2):
            result[s] += jnp.dot(
                act, w_out[:, s * width : (s + 1) * width], preferred_element_type=F32
            )
            part[s] += lax.dot_general(
                act_grad, w_in[s * width : (s + 1) * width, :], NT, preferred_element_type=F32
            )
    blocks = out_ref.shape[0] // 2
    cols = out_ref.shape[2]
    for index in range(blocks):
        side, at = divmod(index, blocks // 2)
        out_ref[index] = result[side][:, at * cols : (at + 1) * cols].astype(BF16)
        out_ref[blocks + index] = part[side][:, at * cols : (at + 1) * cols].astype(BF16)


def grads_kernel(
    dp_ref, rows_ref, act_ref, act_grad_ref, own_in, own_out, send_a, send_b, send_c, hid, grad
):
    gather_columns(rows_ref, hid, grad)
    mine = dp_ref[0]
    hidden = act_ref.shape[2]
    sends = [send_a, send_b, send_c]
    for which in range(2):
        for other in range(2):
            side = mine if other == 0 else 1 - mine
            g_in = lax.dot_general(hid[side], act_grad_ref[which], TN, preferred_element_type=F32)
            g_out = lax.dot_general(act_ref[which], grad[side], TN, preferred_element_type=F32)
            if which == 0 and other == 0:
                own_in[...] = g_in
                own_out[...] = g_out
            else:
                width = g_in.shape[0]
                send = sends.pop(0)
                send[:width] = g_in.astype(BF16)
                for piece in range(g_out.shape[1] // hidden):
                    send[width + piece * hidden : width + (piece + 1) * hidden] = g_out[
                        :, piece * hidden : (piece + 1) * hidden
                    ].astype(BF16)


def vmem(count):
    return [pl.BlockSpec(memory_space=pltpu.VMEM)] * count


def expert_rows(rows, win, win_other, wout, wout_other):
    parts, count, cols = rows.shape
    width = parts * cols // 2
    hidden = win.shape[1]
    flops = 16 * count * width * hidden
    return pl.pallas_call(
        expert_kernel,
        out_shape=(
            jax.ShapeDtypeStruct((2, count, hidden), BF16),
            jax.ShapeDtypeStruct((2, count, hidden), BF16),
            jax.ShapeDtypeStruct((parts, count, cols), BF16),
        ),
        in_specs=vmem(5),
        out_specs=tuple(vmem(3)),
        scratch_shapes=[pltpu.VMEM((2, count, width // 2), BF16)] * 2,
        compiler_params=pltpu.CompilerParams(vmem_limit_bytes=40 * 2**20),
        cost_estimate=pl.CostEstimate(flops=flops, bytes_accessed=5 * 2**20, transcendentals=0),
    )(rows, win, win_other, wout, wout_other)


def weight_grads(dp, rows, act, act_grad):
    parts, count, cols = rows.shape
    width = parts * cols // 2
    hidden = act.shape[2]
    return pl.pallas_call(
        grads_kernel,
        out_shape=(
            jax.ShapeDtypeStruct((width // 2, hidden), F32),
            jax.ShapeDtypeStruct((hidden, width // 2), F32),
        )
        + (jax.ShapeDtypeStruct((width, hidden), BF16),) * 3,
        in_specs=[pl.BlockSpec(memory_space=pltpu.SMEM)] + vmem(3),
        out_specs=tuple(vmem(5)),
        scratch_shapes=[pltpu.VMEM((2, count, width // 2), BF16)] * 2,
        compiler_params=pltpu.CompilerParams(vmem_limit_bytes=40 * 2**20),
        cost_estimate=pl.CostEstimate(
            flops=8 * count * width * hidden, bytes_accessed=5 * 2**20, transcendentals=0
        ),
    )(dp, rows, act, act_grad)


def glu_specs(frames, cols, blocks, place):
    def spec(rows, shift):
        return pl.BlockSpec((rows, cols), lambda i, *ref: (0, shift + place(i, *ref)))

    return [spec(rows, shift) for rows in (frames, RIM, RIM) for shift in (0, blocks)]


def dispatch_rows(where, glu_in, before, after, taps, resid, out_grad, dest, scale, total, cols):
    frames, width = resid.shape
    blocks = width // cols

    def place(i, ref):
        return ref[1]

    def spec(rows):
        return pl.BlockSpec((rows, cols), lambda i, ref: (0, place(i, ref)))

    whole = pl.BlockSpec((1, 2 * frames), lambda i, ref: (0, 0))
    return pl.pallas_call(
        dispatch_kernel,
        out_shape=jax.ShapeDtypeStruct((total, cols), BF16),
        grid_spec=pltpu.PrefetchScalarGridSpec(
            num_scalar_prefetch=1,
            grid=(1,),
            in_specs=glu_specs(frames, cols, blocks, place)
            + [spec(KERNEL), spec(frames), spec(frames), whole, whole],
            out_specs=pl.BlockSpec((total, cols), lambda i, ref: (0, 0)),
            scratch_shapes=[pltpu.VMEM((frames + 2 * RIM, cols), F32)],
        ),
        compiler_params=pltpu.CompilerParams(vmem_limit_bytes=16 * 2**20),
        cost_estimate=pl.CostEstimate(flops=2 * 10**7, bytes_accessed=2**20, transcendentals=0),
    )(where, glu_in, glu_in, before, before, after, after, taps, resid, out_grad, dest, scale)


def column(rows, cols):
    return pl.BlockSpec((rows, cols), lambda i: (0, i))


def forward_full(glu_in, before, after, taps, resid, cols):
    frames, width = resid.shape
    blocks = width // cols
    return pl.pallas_call(
        forward_kernel,
        grid=(blocks,),
        out_shape=(
            jax.ShapeDtypeStruct((frames, width), BF16),
            jax.ShapeDtypeStruct((frames, width), F32),
        ),
        in_specs=glu_specs(frames, cols, blocks, lambda i: i)
        + [column(KERNEL, cols), column(frames, cols)],
        out_specs=(column(frames, cols), column(frames, cols)),
        scratch_shapes=[pltpu.VMEM((frames + 2 * RIM, cols), F32)],
        compiler_params=pltpu.CompilerParams(vmem_limit_bytes=16 * 2**20),
        cost_estimate=pl.CostEstimate(flops=2 * 10**7, bytes_accessed=2**21, transcendentals=0),
    )(glu_in, glu_in, before, before, after, after, taps, resid)


def edge_rows(summed, out_grad, slope):
    blocks, frames, cols = summed.shape
    blocks //= 2
    width = blocks * cols
    last = frames // RIM - 1
    row = pl.BlockSpec((RIM, width), lambda i: (i * last, 0))
    return pl.pallas_call(
        edges_kernel,
        grid=(2,),
        out_shape=jax.ShapeDtypeStruct((2 * RIM, width), BF16),
        in_specs=[pl.BlockSpec((blocks, RIM, cols), lambda i: (1, i * last, 0)), row, row],
        out_specs=pl.BlockSpec((RIM, width), lambda i: (i, 0)),
        compiler_params=pltpu.CompilerParams(vmem_limit_bytes=16 * 2**20),
        cost_estimate=pl.CostEstimate(flops=10**5, bytes_accessed=2**18, transcendentals=0),
    )(summed, out_grad, slope)


def finish(summed, hidden_in, out_grad, slope):
    blocks, frames, cols = summed.shape
    blocks //= 2
    width = blocks * cols
    return pl.pallas_call(
        outputs_kernel,
        grid=(blocks,),
        out_shape=(
            jax.ShapeDtypeStruct((frames, width), BF16),
            jax.ShapeDtypeStruct((frames, width), BF16),
            jax.ShapeDtypeStruct((frames, width), F32),
        ),
        in_specs=[
            pl.BlockSpec((1, frames, cols), lambda i: (i, 0, 0)),
            pl.BlockSpec((1, frames, cols), lambda i: (blocks + i, 0, 0)),
        ]
        + [column(frames, cols)] * 3,
        out_specs=(column(frames, cols),) * 3,
        compiler_params=pltpu.CompilerParams(vmem_limit_bytes=16 * 2**20),
        cost_estimate=pl.CostEstimate(flops=10**6, bytes_accessed=2**21, transcendentals=0),
    )(summed, summed, hidden_in, out_grad, slope)


def backward_full(conv_grad, before, after, taps, glu_in, cols):
    frames = conv_grad.shape[0]
    return pl.pallas_call(
        backward_kernel,
        out_shape=jax.ShapeDtypeStruct(glu_in.shape, BF16),
        in_specs=vmem(5),
        out_specs=pl.BlockSpec(memory_space=pltpu.VMEM),
        scratch_shapes=[pltpu.VMEM((frames + 2 * RIM, cols), F32)],
        compiler_params=pltpu.CompilerParams(vmem_limit_bytes=16 * 2**20),
        cost_estimate=pl.CostEstimate(flops=2 * 10**7, bytes_accessed=2**21, transcendentals=0),
    )(conv_grad, before, after, taps, glu_in)


def shards(resid, glu_input, dw_kernel, w_in, w_out, expert_ids, mix_weights, frame_kept, out_grad):
    frames = resid.shape[1]
    width = resid.shape[2]
    experts = lax.axis_size("tm")
    ranks = lax.axis_size("y")
    capacity = 4 * frames // experts
    half_cap = capacity // 2
    cols = width // ranks
    xl = lax.axis_index("xl")
    y = lax.axis_index("y")
    dp = lax.axis_index("dp")
    weight_in = w_in[0]
    weight_out = w_out[0]
    swap = [(0, 1), (1, 0)]

    glu_in = glu_input[0]
    before, after = rims(glu_in[:RIM], glu_in[frames - RIM :])

    ids = expert_ids[0].T.reshape(-1)
    order = 2 * (jnp.arange(2 * frames) % frames) + jnp.arange(2 * frames) // frames
    earlier = (ids[:, None] == ids[None, :]) & (order[None, :] < order[:, None])
    slot = jnp.sum(earlier.astype(jnp.int32), axis=1)
    dest = ids * capacity + slot
    scale = (mix_weights[0] * frame_kept[0][:, None].astype(F32)).T.reshape(-1)
    pick = (dest[:, None] == jnp.arange(experts * capacity)[None, :]).astype(BF16)
    pick_scale = jnp.where(xl == 0, scale, 1.0)

    rows = dispatch_rows(
        jnp.stack([xl, y]),
        glu_in,
        before,
        after,
        dw_kernel,
        resid[0],
        out_grad[0],
        dest[None],
        scale[None],
        experts * capacity,
        cols,
    )
    rows = lax.all_to_all(rows.reshape(experts, capacity, cols), "tm", 0, 0, tiled=True)
    hidden_in, slope = forward_full(glu_in, before, after, dw_kernel, resid[0], cols)
    win_other = lax.ppermute(weight_in, "xl", swap)
    wout_other = lax.ppermute(weight_out, "xl", swap)
    rows, win_other, wout_other = lax.optimization_barrier((rows, win_other, wout_other))
    rows = rows.reshape(experts, 2, half_cap, cols).transpose(1, 0, 2, 3)
    rows = rows.reshape(2, 1, experts * half_cap, cols)
    rows = jnp.broadcast_to(rows, (2, ranks) + rows.shape[2:]).reshape((-1,) + rows.shape[2:])
    rows = lax.all_to_all(rows, ("xl", "y"), 0, 0, tiled=True)

    act, act_grad, parts = expert_rows(rows, weight_in, win_other, weight_out, wout_other)
    parts = lax.all_to_all(parts, ("xl", "y"), 0, 0, tiled=True)
    own_in, own_out, *send = weight_grads(dp.reshape(1), rows, act, act_grad)
    got = (
        lax.ppermute(send[0], "dp", swap),
        lax.ppermute(send[1], "xl", swap),
        lax.ppermute(send[2], ("xl", "dp"), [(0, 3), (3, 0), (1, 2), (2, 1)]),
    )

    parts = parts.reshape(2, ranks, experts, half_cap, cols).astype(F32).sum(axis=1)
    parts = parts.astype(BF16).transpose(1, 0, 2, 3).reshape(experts, capacity, cols)
    parts = lax.all_to_all(parts, "tm", 0, 0, tiled=True).reshape(experts * capacity, cols)
    picked = jnp.dot(pick, parts, preferred_element_type=F32) * pick_scale[:, None]
    summed = (picked[:frames] + picked[frames:]).astype(BF16)
    summed = lax.all_to_all(
        jnp.broadcast_to(summed[None], (2 * ranks,) + summed.shape), ("xl", "y"), 0, 0, tiled=True
    )

    edges = edge_rows(summed, out_grad[0], slope)
    before, after = rims(edges[:RIM], edges[RIM:])
    block_out, resid_grad, conv_grad = finish(summed, hidden_in, out_grad[0], slope)
    glu_grad = backward_full(conv_grad, before, after, dw_kernel, glu_in, cols)

    hidden = weight_in.shape[1]
    w_in_grad = own_in + sum(piece[: width // 2].astype(F32) for piece in got)
    rest = [
        piece[width // 2 :].reshape(-1, hidden, hidden).transpose(1, 0, 2).reshape(hidden, -1)
        for piece in got
    ]
    w_out_grad = own_out + sum(piece.astype(F32) for piece in rest)
    return (
        block_out[None],
        resid_grad[None],
        glu_grad[None],
        w_in_grad[None],
        w_out_grad[None],
    )


def solution(mesh):
    size = mesh.shape["expert"]
    axes = {"tm": mesh.shape["tm"], "xl": 2, "y": size // 2, "dp": mesh.shape["dp"]}
    split = Mesh(mesh.devices.reshape(tuple(axes.values())), tuple(axes))
    expert = ("xl", "y")
    return jax.shard_map(
        shards,
        mesh=split,
        in_specs=(
            P("dp", "tm", None),
            P("dp", "tm", None),
            P(),
            P("tm", None, expert),
            P("tm", expert, None),
            P("dp", "tm", None),
            P("dp", "tm", None),
            P("dp", "tm"),
            P("dp", "tm", None),
        ),
        out_specs=(
            P("dp", "tm", None),
            P("dp", "tm", None),
            P("dp", "tm", None),
            P("tm", "dp", expert),
            P("tm", expert, "dp"),
        ),
        check_vma=False,
    )
```

```python
import functools

import jax
import jax.numpy as jnp
from jax import lax
from jax.experimental import pallas as pl
from jax.experimental.pallas import tpu as pltpu
from jax.sharding import Mesh, PartitionSpec as P

KERNEL = 31
HALF = KERNEL // 2
F32 = jnp.float32
BF16 = jnp.bfloat16
NT = (((1,), (1,)), ((), ()))
TN = (((0,), (0,)), ((), ()))


RIM = 16


def swish_slope(value):
    sig = jax.nn.sigmoid(value)
    return sig * (1.0 + value * (1.0 - sig))


def rims(top, bottom):
    size = lax.axis_size("tm")
    up = [(i, i + 1) for i in range(size - 1)]
    down = [(j, i) for i, j in up]
    return lax.ppermute(bottom, "tm", up), lax.ppermute(top, "tm", down)


def taps_sum(padded, taps, frames, start, step):
    total = None
    for residue in range(8):
        offsets = [(start + step * j, j) for j in range(KERNEL) if (start + step * j) % 8 == residue]
        reach = max(offset for offset, _ in offsets) - residue
        shifted = padded[residue : residue + reach + frames, :]
        for offset, j in offsets:
            base = offset - residue
            term = taps[j : j + 1, :] * shifted[base : base + frames]
            total = term if total is None else total + term
    return total


def glu(value, gate):
    return value.astype(F32) * jax.nn.sigmoid(gate.astype(F32))


def glu_conv(value, gate, before_value, before_gate, after_value, after_gate, taps, padded):
    frames = value.shape[0]
    padded[:RIM] = glu(before_value[...], before_gate[...])
    padded[RIM : RIM + frames] = glu(value[...], gate[...])
    padded[RIM + frames :] = glu(after_value[...], after_gate[...])
    return taps_sum(padded, taps, frames, RIM - HALF, 1)


def dispatch_kernel(
    experts,
    where_ref,
    value,
    gate,
    before_value,
    before_gate,
    after_value,
    after_gate,
    taps,
    resid,
    out_grad,
    ids,
    mix,
    kept,
    rows_ref,
    dest_ref,
    padded,
):
    frames = value.shape[0]
    total = rows_ref.shape[0]
    conv = glu_conv(value, gate, before_value, before_gate, after_value, after_gate, taps, padded)
    hidden_in = (resid[...].astype(F32) + conv * jax.nn.sigmoid(conv)).astype(BF16)
    first = where_ref[0] == 0
    chosen = jnp.where(first, hidden_in.astype(F32), out_grad[...].astype(F32)).astype(BF16)
    expert = lax.broadcasted_iota(jnp.int32, (experts, frames), 0)
    named = [jnp.where(ids[k : k + 1, :] == expert, 1.0, 0.0) for k in range(2)]
    earlier = lax.broadcasted_iota(jnp.int32, (frames, frames), 0) < lax.broadcasted_iota(
        jnp.int32, (frames, frames), 1
    )
    ahead = jnp.dot(
        (named[0] + named[1]).astype(BF16),
        jnp.where(earlier, 1.0, 0.0).astype(BF16),
        preferred_element_type=F32,
    )
    row = lax.broadcasted_iota(jnp.int32, (total, frames), 0)
    ones = jnp.zeros((total, frames), F32)
    factor = jnp.zeros((total, frames), F32)
    for k in range(2):
        slot = jnp.sum(named[k] * ahead, axis=0, keepdims=True).astype(jnp.int32)
        dest = ids[k : k + 1, :] * (total // experts) + slot
        dest_ref[k : k + 1, :] = dest
        hot = row == dest
        scale = mix[k : k + 1, :] * kept[...].astype(F32)
        ones = jnp.where(hot, 1.0, ones)
        factor = jnp.where(hot, scale, factor)
    ones = ones.astype(BF16)
    factor = jnp.sum(factor, axis=1, keepdims=True)
    rows = jnp.dot(ones, chosen, preferred_element_type=F32)
    rows_ref[...] = jnp.where(first, rows, rows * factor).astype(BF16)


def forward_kernel(
    value,
    gate,
    before_value,
    before_gate,
    after_value,
    after_gate,
    taps,
    resid,
    hidden_ref,
    slope_ref,
    padded,
):
    conv = glu_conv(value, gate, before_value, before_gate, after_value, after_gate, taps, padded)
    sig = jax.nn.sigmoid(conv)
    hidden_ref[...] = (resid[...].astype(F32) + conv * sig).astype(BF16)
    slope_ref[...] = sig * (1.0 + conv * (1.0 - sig))


def edges_kernel(part_ref, out_grad, slope, edges_ref):
    for at in range(part_ref.shape[0]):
        cols = slice(at * part_ref.shape[2], (at + 1) * part_ref.shape[2])
        hid_grad = out_grad[:, cols].astype(F32) + part_ref[at].astype(F32)
        edges_ref[:, cols] = (hid_grad * slope[:, cols]).astype(BF16)


def outputs_kernel(summed, hidden, out_grad, slope, block_ref, resid_ref, conv_grad_ref):
    blocks = summed.shape[0] // 2
    for at in range(blocks):
        cols = slice(at * summed.shape[2], (at + 1) * summed.shape[2])
        moe = summed[at].astype(F32)
        block_ref[:, cols] = (hidden[:, cols].astype(F32) + moe).astype(BF16)
        hid_grad = out_grad[:, cols].astype(F32) + summed[blocks + at].astype(F32)
        resid_ref[:, cols] = hid_grad.astype(BF16)
        conv_grad_ref[:, cols] = hid_grad * slope[:, cols]


def backward_kernel(conv_grad, before, after, taps, glu_in, out, padded):
    frames, width = conv_grad.shape
    cols = padded.shape[1]

    def step(index, carry):
        at = pl.ds(pl.multiple_of(index * cols, cols), cols)
        at_gate = pl.ds(pl.multiple_of(width + index * cols, cols), cols)
        padded[:RIM] = before[:, at].astype(F32)
        padded[RIM : RIM + frames] = conv_grad[:, at]
        padded[RIM + frames :] = after[:, at].astype(F32)
        back = taps_sum(padded, taps[:, at], frames, RIM + HALF, -1)
        sig = jax.nn.sigmoid(glu_in[:, at_gate].astype(F32))
        grad = back * sig
        out[:, at] = grad.astype(BF16)
        out[:, at_gate] = (grad * glu_in[:, at].astype(F32) * (1.0 - sig)).astype(BF16)
        return carry

    lax.fori_loop(0, width // cols, step, 0)


def gather_columns(rows_ref, hid, grad):
    parts = rows_ref.shape[0] // 2
    cols = rows_ref.shape[2]
    for part in range(parts):
        side, at = divmod(part, parts // 2)
        hid[side, :, at * cols : (at + 1) * cols] = rows_ref[part]
        grad[side, :, at * cols : (at + 1) * cols] = rows_ref[parts + part]


def expert_kernel(rows_ref, win_a, win_b, wout_a, wout_b, act_ref, act_grad_ref, out_ref, hid, grad):
    gather_columns(rows_ref, hid, grad)
    width = hid.shape[2]
    result = [0.0, 0.0]
    part = [0.0, 0.0]
    for which, (w_in, w_out) in enumerate(((win_a, wout_a), (win_b, wout_b))):
        pre = sum(
            jnp.dot(hid[s], w_in[s * width : (s + 1) * width, :], preferred_element_type=F32)
            for s in range(2)
        )
        back = sum(
            lax.dot_general(
                grad[s], w_out[:, s * width : (s + 1) * width], NT, preferred_element_type=F32
            )
            for s in range(2)
        )
        sig = jax.nn.sigmoid(pre)
        act = (pre * sig).astype(BF16)
        act_grad = (back * (sig * (1.0 + pre * (1.0 - sig)))).astype(BF16)
        act_ref[which] = act
        act_grad_ref[which] = act_grad
        for s in range(2):
            result[s] += jnp.dot(
                act, w_out[:, s * width : (s + 1) * width], preferred_element_type=F32
            )
            part[s] += lax.dot_general(
                act_grad, w_in[s * width : (s + 1) * width, :], NT, preferred_element_type=F32
            )
    blocks = out_ref.shape[0] // 2
    cols = out_ref.shape[2]
    for index in range(blocks):
        side, at = divmod(index, blocks // 2)
        out_ref[index] = result[side][:, at * cols : (at + 1) * cols].astype(BF16)
        out_ref[blocks + index] = part[side][:, at * cols : (at + 1) * cols].astype(BF16)


def grads_kernel(pieces, dp_ref, rows_ref, act_ref, act_grad_ref, *refs):
    *outs, hid, grad = refs
    gather_columns(rows_ref, hid, grad)
    mine = dp_ref[0]
    hidden = act_ref.shape[2]
    for which, other in pieces:
        side = mine if other == 0 else 1 - mine
        g_in = lax.dot_general(hid[side], act_grad_ref[which], TN, preferred_element_type=F32)
        g_out = lax.dot_general(act_ref[which], grad[side], TN, preferred_element_type=F32)
        if which == 0 and other == 0:
            own_in, own_out, *outs = outs
            own_in[...] = g_in
            own_out[...] = g_out
        else:
            width = g_in.shape[0]
            send, *outs = outs
            send[:width] = g_in.astype(BF16)
            for piece in range(g_out.shape[1] // hidden):
                send[width + piece * hidden : width + (piece + 1) * hidden] = g_out[
                    :, piece * hidden : (piece + 1) * hidden
                ].astype(BF16)


def vmem(count):
    return [pl.BlockSpec(memory_space=pltpu.VMEM)] * count


def expert_rows(rows, win, win_other, wout, wout_other):
    parts, count, cols = rows.shape
    width = parts * cols // 2
    hidden = win.shape[1]
    flops = 16 * count * width * hidden
    return pl.pallas_call(
        expert_kernel,
        out_shape=(
            jax.ShapeDtypeStruct((2, count, hidden), BF16),
            jax.ShapeDtypeStruct((2, count, hidden), BF16),
            jax.ShapeDtypeStruct((parts, count, cols), BF16),
        ),
        in_specs=vmem(5),
        out_specs=tuple(vmem(3)),
        scratch_shapes=[pltpu.VMEM((2, count, width // 2), BF16)] * 2,
        compiler_params=pltpu.CompilerParams(vmem_limit_bytes=40 * 2**20),
        cost_estimate=pl.CostEstimate(flops=flops, bytes_accessed=5 * 2**20, transcendentals=0),
    )(rows, win, win_other, wout, wout_other)


def weight_grads(pieces, dp, rows, act, act_grad):
    parts, count, cols = rows.shape
    width = parts * cols // 2
    hidden = act.shape[2]
    shapes = []
    for piece in pieces:
        if piece == (0, 0):
            shapes.append(jax.ShapeDtypeStruct((width // 2, hidden), F32))
            shapes.append(jax.ShapeDtypeStruct((hidden, width // 2), F32))
        else:
            shapes.append(jax.ShapeDtypeStruct((width, hidden), BF16))
    return pl.pallas_call(
        functools.partial(grads_kernel, pieces),
        out_shape=tuple(shapes),
        in_specs=[pl.BlockSpec(memory_space=pltpu.SMEM)] + vmem(3),
        out_specs=tuple(vmem(len(shapes))),
        scratch_shapes=[pltpu.VMEM((2, count, width // 2), BF16)] * 2,
        compiler_params=pltpu.CompilerParams(vmem_limit_bytes=40 * 2**20),
        cost_estimate=pl.CostEstimate(
            flops=2 * len(pieces) * count * width * hidden,
            bytes_accessed=4 * 2**20,
            transcendentals=0,
        ),
    )(dp, rows, act, act_grad)


def glu_specs(frames, cols, blocks, place):
    def spec(rows, shift):
        return pl.BlockSpec((rows, cols), lambda i, *ref: (0, shift + place(i, *ref)))

    return [spec(rows, shift) for rows in (frames, RIM, RIM) for shift in (0, blocks)]


def dispatch_rows(
    where, glu_in, before, after, taps, resid, out_grad, ids, mix, kept, experts, total, cols
):
    frames, width = resid.shape
    blocks = width // cols

    def place(i, ref):
        return ref[1]

    def spec(rows):
        return pl.BlockSpec((rows, cols), lambda i, ref: (0, place(i, ref)))

    def whole(rows, columns):
        return pl.BlockSpec((rows, columns), lambda i, ref: (0, 0))

    return pl.pallas_call(
        functools.partial(dispatch_kernel, experts),
        out_shape=(
            jax.ShapeDtypeStruct((total, cols), BF16),
            jax.ShapeDtypeStruct((2, frames), jnp.int32),
        ),
        grid_spec=pltpu.PrefetchScalarGridSpec(
            num_scalar_prefetch=1,
            grid=(1,),
            in_specs=glu_specs(frames, cols, blocks, place)
            + [spec(KERNEL), spec(frames), spec(frames)]
            + [whole(2, frames), whole(2, frames), whole(1, frames)],
            out_specs=(whole(total, cols), whole(2, frames)),
            scratch_shapes=[pltpu.VMEM((frames + 2 * RIM, cols), F32)],
        ),
        compiler_params=pltpu.CompilerParams(vmem_limit_bytes=56 * 2**20),
        cost_estimate=pl.CostEstimate(flops=2 * 10**7, bytes_accessed=2**20, transcendentals=0),
    )(where, glu_in, glu_in, before, before, after, after, taps, resid, out_grad, ids, mix, kept)


def column(rows, cols):
    return pl.BlockSpec((rows, cols), lambda i: (0, i))


def forward_full(glu_in, before, after, taps, resid, cols):
    frames, width = resid.shape
    blocks = width // cols
    return pl.pallas_call(
        forward_kernel,
        grid=(blocks,),
        out_shape=(
            jax.ShapeDtypeStruct((frames, width), BF16),
            jax.ShapeDtypeStruct((frames, width), F32),
        ),
        in_specs=glu_specs(frames, cols, blocks, lambda i: i)
        + [column(KERNEL, cols), column(frames, cols)],
        out_specs=(column(frames, cols), column(frames, cols)),
        scratch_shapes=[pltpu.VMEM((frames + 2 * RIM, cols), F32)],
        compiler_params=pltpu.CompilerParams(vmem_limit_bytes=16 * 2**20),
        cost_estimate=pl.CostEstimate(flops=2 * 10**7, bytes_accessed=2**21, transcendentals=0),
    )(glu_in, glu_in, before, before, after, after, taps, resid)


def edge_rows(summed, out_grad, slope):
    blocks, frames, cols = summed.shape
    blocks //= 2
    width = blocks * cols
    last = frames // RIM - 1
    row = pl.BlockSpec((RIM, width), lambda i: (i * last, 0))
    return pl.pallas_call(
        edges_kernel,
        grid=(2,),
        out_shape=jax.ShapeDtypeStruct((2 * RIM, width), BF16),
        in_specs=[pl.BlockSpec((blocks, RIM, cols), lambda i: (1, i * last, 0)), row, row],
        out_specs=pl.BlockSpec((RIM, width), lambda i: (i, 0)),
        compiler_params=pltpu.CompilerParams(vmem_limit_bytes=16 * 2**20),
        cost_estimate=pl.CostEstimate(flops=10**5, bytes_accessed=2**18, transcendentals=0),
    )(summed, out_grad, slope)


def finish(summed, hidden_in, out_grad, slope):
    half = jax.ShapeDtypeStruct(hidden_in.shape, BF16)
    return pl.pallas_call(
        outputs_kernel,
        out_shape=(half, half, jax.ShapeDtypeStruct(hidden_in.shape, F32)),
        in_specs=vmem(4),
        out_specs=tuple(vmem(3)),
        compiler_params=pltpu.CompilerParams(vmem_limit_bytes=16 * 2**20),
        cost_estimate=pl.CostEstimate(flops=10**6, bytes_accessed=2**21, transcendentals=0),
    )(summed, hidden_in, out_grad, slope)


def backward_full(conv_grad, before, after, taps, glu_in, cols):
    frames = conv_grad.shape[0]
    return pl.pallas_call(
        backward_kernel,
        out_shape=jax.ShapeDtypeStruct(glu_in.shape, BF16),
        in_specs=vmem(5),
        out_specs=pl.BlockSpec(memory_space=pltpu.VMEM),
        scratch_shapes=[pltpu.VMEM((frames + 2 * RIM, cols), F32)],
        compiler_params=pltpu.CompilerParams(vmem_limit_bytes=16 * 2**20),
        cost_estimate=pl.CostEstimate(flops=2 * 10**7, bytes_accessed=2**21, transcendentals=0),
    )(conv_grad, before, after, taps, glu_in)


def shards(resid, glu_input, dw_kernel, w_in, w_out, expert_ids, mix_weights, frame_kept, out_grad):
    frames = resid.shape[1]
    width = resid.shape[2]
    experts = lax.axis_size("tm")
    ranks = lax.axis_size("y")
    capacity = 4 * frames // experts
    half_cap = capacity // 2
    cols = width // ranks
    xl = lax.axis_index("xl")
    y = lax.axis_index("y")
    dp = lax.axis_index("dp")
    weight_in = w_in[0]
    weight_out = w_out[0]
    swap = [(0, 1), (1, 0)]
    swap_both = [(0, 3), (3, 0), (1, 2), (2, 1)]

    glu_in = glu_input[0]
    before, after = rims(glu_in[:RIM], glu_in[frames - RIM :])

    ids = expert_ids[0].T
    mix = mix_weights[0].T
    rows, dest = dispatch_rows(
        jnp.stack([xl, y]),
        glu_in,
        before,
        after,
        dw_kernel,
        resid[0],
        out_grad[0],
        ids,
        mix,
        frame_kept,
        experts,
        experts * capacity,
        cols,
    )
    rows = lax.all_to_all(rows.reshape(experts, capacity, cols), "tm", 0, 0, tiled=True)
    hidden_in, slope = forward_full(glu_in, before, after, dw_kernel, resid[0], cols)
    win_other = lax.ppermute(weight_in, "xl", swap)
    wout_other = lax.ppermute(weight_out, ("xl", "dp"), swap_both)
    rows = rows.reshape(experts, 2, half_cap, cols).transpose(1, 0, 2, 3)
    rows = rows.reshape(2, 1, experts * half_cap, cols)
    rows = jnp.broadcast_to(rows, (2, ranks) + rows.shape[2:]).reshape((-1,) + rows.shape[2:])
    rows = lax.all_to_all(rows, ("xl", "y"), 0, 0, tiled=True)

    act, act_grad, parts = expert_rows(rows, weight_in, win_other, weight_out, wout_other)
    parts = lax.all_to_all(parts, ("xl", "y"), 0, 0, tiled=True)
    pieces = [(0, 0), (0, 1), (1, 0), (1, 1)]
    own_in, own_out, *send = weight_grads(pieces, dp.reshape(1), rows, act, act_grad)
    got_both = lax.ppermute(send[2], ("xl", "dp"), swap_both)
    got_xl = lax.ppermute(send[1], "xl", swap)
    got_dp = lax.ppermute(send[0], "dp", swap)
    parts, got_both, got_xl = lax.optimization_barrier((parts, got_both, got_xl))

    parts = parts.reshape(2, ranks, experts, half_cap, cols).astype(F32).sum(axis=1)
    parts = parts.astype(BF16).transpose(1, 0, 2, 3).reshape(experts, capacity, cols)
    parts = lax.all_to_all(parts, "tm", 0, 0, tiled=True).reshape(experts * capacity, cols)
    parts, got_dp = lax.optimization_barrier((parts, got_dp))
    got = (got_dp, got_xl, got_both)
    scale = (mix * frame_kept.astype(F32)).reshape(-1)
    pick = (dest.reshape(-1)[:, None] == jnp.arange(experts * capacity)[None, :]).astype(BF16)
    pick_scale = jnp.where(xl == 0, scale, 1.0)
    picked = jnp.dot(pick, parts, preferred_element_type=F32) * pick_scale[:, None]
    summed = (picked[:frames] + picked[frames:]).astype(BF16)
    summed = lax.all_to_all(
        jnp.broadcast_to(summed[None], (2 * ranks,) + summed.shape), ("xl", "y"), 0, 0, tiled=True
    )

    edges = edge_rows(summed, out_grad[0], slope)
    before, after = rims(edges[:RIM], edges[RIM:])
    block_out, resid_grad, conv_grad = finish(summed, hidden_in, out_grad[0], slope)
    glu_grad = backward_full(conv_grad, before, after, dw_kernel, glu_in, cols)

    hidden = weight_in.shape[1]
    w_in_grad = own_in + sum(piece[: width // 2].astype(F32) for piece in got)
    rest = [
        piece[width // 2 :].reshape(-1, hidden, hidden).transpose(1, 0, 2).reshape(hidden, -1)
        for piece in got
    ]
    w_out_grad = own_out + sum(piece.astype(F32) for piece in rest)
    return (
        block_out[None],
        resid_grad[None],
        glu_grad[None],
        w_in_grad[None],
        w_out_grad[None],
    )


def solution(mesh):
    size = mesh.shape["expert"]
    axes = {"tm": mesh.shape["tm"], "xl": 2, "y": size // 2, "dp": mesh.shape["dp"]}
    split = Mesh(mesh.devices.reshape(tuple(axes.values())), tuple(axes))
    expert = ("xl", "y")
    return jax.shard_map(
        shards,
        mesh=split,
        in_specs=(
            P("dp", "tm", None),
            P("dp", "tm", None),
            P(),
            P("tm", None, expert),
            P("tm", expert, None),
            P("dp", "tm", None),
            P("dp", "tm", None),
            P("dp", "tm"),
            P("dp", "tm", None),
        ),
        out_specs=(
            P("dp", "tm", None),
            P("dp", "tm", None),
            P("dp", "tm", None),
            P("tm", "dp", expert),
            P("tm", expert, "dp"),
        ),
        check_vma=False,
    )
```

```python
import functools

import jax
import jax.numpy as jnp
from jax import lax
from jax.experimental import pallas as pl
from jax.experimental.pallas import tpu as pltpu
from jax.sharding import Mesh, PartitionSpec as P

KERNEL = 31
HALF = KERNEL // 2
F32 = jnp.float32
BF16 = jnp.bfloat16
NT = (((1,), (1,)), ((), ()))
TN = (((0,), (0,)), ((), ()))


RIM = 16


def swish_slope(value):
    sig = jax.nn.sigmoid(value)
    return sig * (1.0 + value * (1.0 - sig))


def rims(top, bottom):
    size = lax.axis_size("tm")
    up = [(i, i + 1) for i in range(size - 1)]
    down = [(j, i) for i, j in up]
    return lax.ppermute(bottom, "tm", up), lax.ppermute(top, "tm", down)


def edge_rims(top, bottom, half):
    size = lax.axis_size("tm")
    up = [(2 * i + 1, 2 * (i + 1) + half) for i in range(size - 1)]
    down = [(2 * (i + 1) + 1, 2 * i + half) for i in range(size - 1)]
    return lax.ppermute(bottom, ("tm", "xl"), up), lax.ppermute(top, ("tm", "xl"), down)


def taps_sum(padded, taps, frames, start, step):
    total = None
    for residue in range(8):
        offsets = [(start + step * j, j) for j in range(KERNEL) if (start + step * j) % 8 == residue]
        reach = max(offset for offset, _ in offsets) - residue
        shifted = padded[residue : residue + reach + frames, :]
        for offset, j in offsets:
            base = offset - residue
            term = taps[j : j + 1, :] * shifted[base : base + frames]
            total = term if total is None else total + term
    return total


def glu(value, gate):
    return value.astype(F32) * jax.nn.sigmoid(gate.astype(F32))


def glu_conv(value, gate, before_value, before_gate, after_value, after_gate, taps, padded):
    frames = value.shape[0]
    padded[:RIM] = glu(before_value[...], before_gate[...])
    padded[RIM : RIM + frames] = glu(value[...], gate[...])
    padded[RIM + frames :] = glu(after_value[...], after_gate[...])
    return taps_sum(padded, taps, frames, RIM - HALF, 1)


def dispatch_kernel(
    experts,
    where_ref,
    value,
    gate,
    before_value,
    before_gate,
    after_value,
    after_gate,
    taps,
    resid,
    out_grad,
    ids,
    mix,
    kept,
    rows_ref,
    dest_ref,
    padded,
):
    frames = value.shape[0]
    total = rows_ref.shape[0]
    conv = glu_conv(value, gate, before_value, before_gate, after_value, after_gate, taps, padded)
    hidden_in = (resid[...].astype(F32) + conv * jax.nn.sigmoid(conv)).astype(BF16)
    first = where_ref[0] == 0
    chosen = jnp.where(first, hidden_in.astype(F32), out_grad[...].astype(F32)).astype(BF16)
    expert = lax.broadcasted_iota(jnp.int32, (experts, frames), 0)
    named = [jnp.where(ids[k : k + 1, :] == expert, 1.0, 0.0) for k in range(2)]
    earlier = lax.broadcasted_iota(jnp.int32, (frames, frames), 0) < lax.broadcasted_iota(
        jnp.int32, (frames, frames), 1
    )
    ahead = jnp.dot(
        (named[0] + named[1]).astype(BF16),
        jnp.where(earlier, 1.0, 0.0).astype(BF16),
        preferred_element_type=F32,
    )
    row = lax.broadcasted_iota(jnp.int32, (total, frames), 0)
    ones = jnp.zeros((total, frames), F32)
    factor = jnp.zeros((total, frames), F32)
    for k in range(2):
        slot = jnp.sum(named[k] * ahead, axis=0, keepdims=True).astype(jnp.int32)
        dest = ids[k : k + 1, :] * (total // experts) + slot
        dest_ref[k : k + 1, :] = dest
        hot = row == dest
        scale = mix[k : k + 1, :] * kept[...].astype(F32)
        ones = jnp.where(hot, 1.0, ones)
        factor = jnp.where(hot, scale, factor)
    ones = ones.astype(BF16)
    factor = jnp.sum(factor, axis=1, keepdims=True)
    rows = jnp.dot(ones, chosen, preferred_element_type=F32)
    rows_ref[...] = jnp.where(first, rows, rows * factor).astype(BF16)


def forward_kernel(
    value,
    gate,
    before_value,
    before_gate,
    after_value,
    after_gate,
    taps,
    resid,
    hidden_ref,
    slope_ref,
    padded,
):
    conv = glu_conv(value, gate, before_value, before_gate, after_value, after_gate, taps, padded)
    sig = jax.nn.sigmoid(conv)
    hidden_ref[...] = (resid[...].astype(F32) + conv * sig).astype(BF16)
    slope_ref[...] = sig * (1.0 + conv * (1.0 - sig))


def edges_kernel(part_ref, out_grad, slope, copy_ref, top_ref, bottom_ref):
    copy_ref[...] = part_ref[...]
    frames = out_grad.shape[0]
    for edge, rows in ((top_ref, slice(RIM)), (bottom_ref, slice(frames - RIM, frames))):
        for at in range(part_ref.shape[0]):
            cols = slice(at * part_ref.shape[2], (at + 1) * part_ref.shape[2])
            hid_grad = out_grad[rows, cols].astype(F32) + part_ref[at, rows].astype(F32)
            edge[:, cols] = (hid_grad * slope[rows, cols]).astype(BF16)


def backward_kernel(
    where_ref,
    mine,
    other,
    hidden,
    out_grad,
    slope,
    before_a,
    after_a,
    before_b,
    after_b,
    taps,
    glu_in,
    block_ref,
    resid_ref,
    out,
    padded,
):
    frames, width = out_grad.shape
    cols = padded.shape[1]
    first = where_ref[0] == 0

    def step(index, carry):
        at = pl.ds(pl.multiple_of(index * cols, cols), cols)
        at_gate = pl.ds(pl.multiple_of(width + index * cols, cols), cols)
        here, there = mine[index].astype(F32), other[index].astype(F32)
        moe = jnp.where(first, here, there)
        block_ref[:, at] = (hidden[:, at].astype(F32) + moe).astype(BF16)
        hid_grad = out_grad[:, at].astype(F32) + jnp.where(first, there, here)
        resid_ref[:, at] = hid_grad.astype(BF16)
        padded[:RIM] = before_a[:, at].astype(F32) + before_b[:, at].astype(F32)
        padded[RIM : RIM + frames] = hid_grad * slope[:, at]
        padded[RIM + frames :] = after_a[:, at].astype(F32) + after_b[:, at].astype(F32)
        back = taps_sum(padded, taps[:, at], frames, RIM + HALF, -1)
        sig = jax.nn.sigmoid(glu_in[:, at_gate].astype(F32))
        grad = back * sig
        out[:, at] = grad.astype(BF16)
        out[:, at_gate] = (grad * glu_in[:, at].astype(F32) * (1.0 - sig)).astype(BF16)
        return carry

    lax.fori_loop(0, width // cols, step, 0)


def gather_columns(rows_ref, hid, grad):
    parts = rows_ref.shape[0] // 2
    cols = rows_ref.shape[2]
    for part in range(parts):
        side, at = divmod(part, parts // 2)
        hid[side, :, at * cols : (at + 1) * cols] = rows_ref[part]
        grad[side, :, at * cols : (at + 1) * cols] = rows_ref[parts + part]


def expert_kernel(rows_ref, win_a, win_b, wout_a, wout_b, act_ref, act_grad_ref, out_ref, hid, grad):
    gather_columns(rows_ref, hid, grad)
    width = hid.shape[2]
    result = [0.0, 0.0]
    part = [0.0, 0.0]
    for which, (w_in, w_out) in enumerate(((win_a, wout_a), (win_b, wout_b))):
        pre = sum(
            jnp.dot(hid[s], w_in[s * width : (s + 1) * width, :], preferred_element_type=F32)
            for s in range(2)
        )
        back = sum(
            lax.dot_general(
                grad[s], w_out[:, s * width : (s + 1) * width], NT, preferred_element_type=F32
            )
            for s in range(2)
        )
        sig = jax.nn.sigmoid(pre)
        act = (pre * sig).astype(BF16)
        act_grad = (back * (sig * (1.0 + pre * (1.0 - sig)))).astype(BF16)
        act_ref[which] = act
        act_grad_ref[which] = act_grad
        for s in range(2):
            result[s] += jnp.dot(
                act, w_out[:, s * width : (s + 1) * width], preferred_element_type=F32
            )
            part[s] += lax.dot_general(
                act_grad, w_in[s * width : (s + 1) * width, :], NT, preferred_element_type=F32
            )
    blocks = out_ref.shape[0] // 2
    cols = out_ref.shape[2]
    for index in range(blocks):
        side, at = divmod(index, blocks // 2)
        out_ref[index] = result[side][:, at * cols : (at + 1) * cols].astype(BF16)
        out_ref[blocks + index] = part[side][:, at * cols : (at + 1) * cols].astype(BF16)


def grads_kernel(pieces, dp_ref, rows_ref, act_ref, act_grad_ref, *refs):
    *outs, hid, grad = refs
    gather_columns(rows_ref, hid, grad)
    mine = dp_ref[0]
    hidden = act_ref.shape[2]
    for which, other in pieces:
        side = mine if other == 0 else 1 - mine
        g_in = lax.dot_general(hid[side], act_grad_ref[which], TN, preferred_element_type=F32)
        g_out = lax.dot_general(act_ref[which], grad[side], TN, preferred_element_type=F32)
        if which == 0 and other == 0:
            own_in, own_out, *outs = outs
            own_in[...] = g_in
            own_out[...] = g_out
        else:
            width = g_in.shape[0]
            send, *outs = outs
            send[:width] = g_in.astype(BF16)
            for piece in range(g_out.shape[1] // hidden):
                send[width + piece * hidden : width + (piece + 1) * hidden] = g_out[
                    :, piece * hidden : (piece + 1) * hidden
                ].astype(BF16)


def vmem(count):
    return [pl.BlockSpec(memory_space=pltpu.VMEM)] * count


def expert_rows(rows, win, win_other, wout, wout_other):
    parts, count, cols = rows.shape
    width = parts * cols // 2
    hidden = win.shape[1]
    flops = 16 * count * width * hidden
    return pl.pallas_call(
        expert_kernel,
        out_shape=(
            jax.ShapeDtypeStruct((2, count, hidden), BF16),
            jax.ShapeDtypeStruct((2, count, hidden), BF16),
            jax.ShapeDtypeStruct((parts, count, cols), BF16),
        ),
        in_specs=vmem(5),
        out_specs=tuple(vmem(3)),
        scratch_shapes=[pltpu.VMEM((2, count, width // 2), BF16)] * 2,
        compiler_params=pltpu.CompilerParams(vmem_limit_bytes=40 * 2**20),
        cost_estimate=pl.CostEstimate(flops=flops, bytes_accessed=5 * 2**20, transcendentals=0),
    )(rows, win, win_other, wout, wout_other)


def weight_grads(pieces, dp, rows, act, act_grad):
    parts, count, cols = rows.shape
    width = parts * cols // 2
    hidden = act.shape[2]
    shapes = []
    for piece in pieces:
        if piece == (0, 0):
            shapes.append(jax.ShapeDtypeStruct((width // 2, hidden), F32))
            shapes.append(jax.ShapeDtypeStruct((hidden, width // 2), F32))
        else:
            shapes.append(jax.ShapeDtypeStruct((width, hidden), BF16))
    return pl.pallas_call(
        functools.partial(grads_kernel, pieces),
        out_shape=tuple(shapes),
        in_specs=[pl.BlockSpec(memory_space=pltpu.SMEM)] + vmem(3),
        out_specs=tuple(vmem(len(shapes))),
        scratch_shapes=[pltpu.VMEM((2, count, width // 2), BF16)] * 2,
        compiler_params=pltpu.CompilerParams(vmem_limit_bytes=40 * 2**20),
        cost_estimate=pl.CostEstimate(
            flops=2 * len(pieces) * count * width * hidden,
            bytes_accessed=4 * 2**20,
            transcendentals=0,
        ),
    )(dp, rows, act, act_grad)


def glu_specs(frames, cols, blocks, place):
    def spec(rows, shift):
        return pl.BlockSpec((rows, cols), lambda i, *ref: (0, shift + place(i, *ref)))

    return [spec(rows, shift) for rows in (frames, RIM, RIM) for shift in (0, blocks)]


def dispatch_rows(
    where, glu_in, before, after, taps, resid, out_grad, ids, mix, kept, experts, total, cols
):
    frames, width = resid.shape
    blocks = width // cols

    def place(i, ref):
        return ref[1]

    def spec(rows):
        return pl.BlockSpec((rows, cols), lambda i, ref: (0, place(i, ref)))

    def whole(rows, columns):
        return pl.BlockSpec((rows, columns), lambda i, ref: (0, 0))

    return pl.pallas_call(
        functools.partial(dispatch_kernel, experts),
        out_shape=(
            jax.ShapeDtypeStruct((total, cols), BF16),
            jax.ShapeDtypeStruct((2, frames), jnp.int32),
        ),
        grid_spec=pltpu.PrefetchScalarGridSpec(
            num_scalar_prefetch=1,
            grid=(1,),
            in_specs=glu_specs(frames, cols, blocks, place)
            + [spec(KERNEL), spec(frames), spec(frames)]
            + [whole(2, frames), whole(2, frames), whole(1, frames)],
            out_specs=(whole(total, cols), whole(2, frames)),
            scratch_shapes=[pltpu.VMEM((frames + 2 * RIM, cols), F32)],
        ),
        compiler_params=pltpu.CompilerParams(vmem_limit_bytes=56 * 2**20),
        cost_estimate=pl.CostEstimate(flops=2 * 10**7, bytes_accessed=2**20, transcendentals=0),
    )(where, glu_in, glu_in, before, before, after, after, taps, resid, out_grad, ids, mix, kept)


def column(rows, cols):
    return pl.BlockSpec((rows, cols), lambda i: (0, i))


def forward_full(glu_in, before, after, taps, resid, cols):
    frames, width = resid.shape
    blocks = width // cols
    return pl.pallas_call(
        forward_kernel,
        grid=(blocks,),
        out_shape=(
            jax.ShapeDtypeStruct((frames, width), BF16),
            jax.ShapeDtypeStruct((frames, width), F32),
        ),
        in_specs=glu_specs(frames, cols, blocks, lambda i: i)
        + [column(KERNEL, cols), column(frames, cols)],
        out_specs=(column(frames, cols), column(frames, cols)),
        scratch_shapes=[pltpu.VMEM((frames + 2 * RIM, cols), F32)],
        compiler_params=pltpu.CompilerParams(vmem_limit_bytes=16 * 2**20),
        cost_estimate=pl.CostEstimate(flops=2 * 10**7, bytes_accessed=2**21, transcendentals=0),
    )(glu_in, glu_in, before, before, after, after, taps, resid)


def edge_rows(part, out_grad, slope):
    rim = jax.ShapeDtypeStruct((RIM, out_grad.shape[1]), BF16)
    return pl.pallas_call(
        edges_kernel,
        out_shape=(jax.ShapeDtypeStruct(part.shape, BF16), rim, rim),
        in_specs=vmem(3),
        out_specs=tuple(vmem(3)),
        compiler_params=pltpu.CompilerParams(vmem_limit_bytes=16 * 2**20),
        cost_estimate=pl.CostEstimate(flops=10**5, bytes_accessed=2**18, transcendentals=0),
    )(part, out_grad, slope)


def backward_full(where, mine, other, hidden_in, out_grad, slope, halos, taps, glu_in):
    cols = mine.shape[2]
    frames = out_grad.shape[0]
    half = jax.ShapeDtypeStruct(out_grad.shape, BF16)
    return pl.pallas_call(
        backward_kernel,
        out_shape=(half, half, jax.ShapeDtypeStruct(glu_in.shape, BF16)),
        in_specs=[pl.BlockSpec(memory_space=pltpu.SMEM)] + vmem(7 + len(halos)),
        out_specs=tuple(vmem(3)),
        scratch_shapes=[pltpu.VMEM((frames + 2 * RIM, cols), F32)],
        compiler_params=pltpu.CompilerParams(vmem_limit_bytes=16 * 2**20),
        cost_estimate=pl.CostEstimate(flops=2 * 10**7, bytes_accessed=2**21, transcendentals=0),
    )(where, mine, other, hidden_in, out_grad, slope, *halos, taps, glu_in)


def shards(resid, glu_input, dw_kernel, w_in, w_out, expert_ids, mix_weights, frame_kept, out_grad):
    frames = resid.shape[1]
    width = resid.shape[2]
    experts = lax.axis_size("tm")
    ranks = lax.axis_size("y")
    capacity = 4 * frames // experts
    half_cap = capacity // 2
    cols = width // ranks
    xl = lax.axis_index("xl")
    y = lax.axis_index("y")
    dp = lax.axis_index("dp")
    weight_in = w_in[0]
    weight_out = w_out[0]
    swap = [(0, 1), (1, 0)]
    swap_both = [(0, 3), (3, 0), (1, 2), (2, 1)]

    glu_in = glu_input[0]
    before, after = rims(glu_in[:RIM], glu_in[frames - RIM :])

    ids = expert_ids[0].T
    mix = mix_weights[0].T
    rows, dest = dispatch_rows(
        jnp.stack([xl, y]),
        glu_in,
        before,
        after,
        dw_kernel,
        resid[0],
        out_grad[0],
        ids,
        mix,
        frame_kept,
        experts,
        experts * capacity,
        cols,
    )
    rows = lax.all_to_all(rows.reshape(experts, capacity, cols), "tm", 0, 0, tiled=True)
    hidden_in, slope = forward_full(glu_in, before, after, dw_kernel, resid[0], cols)
    win_other = lax.ppermute(weight_in, "xl", swap)
    wout_other = lax.ppermute(weight_out, ("xl", "dp"), swap_both)
    rows = rows.reshape(experts, 2, half_cap, cols).transpose(1, 0, 2, 3)
    rows = rows.reshape(2, 1, experts * half_cap, cols)
    rows = jnp.broadcast_to(rows, (2, ranks) + rows.shape[2:]).reshape((-1,) + rows.shape[2:])
    rows = lax.all_to_all(rows, ("xl", "y"), 0, 0, tiled=True)

    act, act_grad, parts = expert_rows(rows, weight_in, win_other, weight_out, wout_other)
    parts = lax.all_to_all(parts, ("xl", "y"), 0, 0, tiled=True)
    pieces = [(0, 0), (0, 1), (1, 0), (1, 1)]
    own_in, own_out, *send = weight_grads(pieces, dp.reshape(1), rows, act, act_grad)
    got_both = lax.ppermute(send[2], ("xl", "dp"), swap_both)
    got_xl = lax.ppermute(send[1], "xl", swap)
    got_dp = lax.ppermute(send[0], "dp", swap)
    parts, got_both = lax.optimization_barrier((parts, got_both))

    parts = parts.reshape(2, ranks, experts, half_cap, cols).astype(F32).sum(axis=1)
    parts = parts.astype(BF16).transpose(1, 0, 2, 3).reshape(experts, capacity, cols)
    parts = lax.all_to_all(parts, "tm", 0, 0, tiled=True).reshape(experts * capacity, cols)
    parts, got_dp, got_xl = lax.optimization_barrier((parts, got_dp, got_xl))
    got = (got_dp, got_xl, got_both)
    scale = (mix * frame_kept.astype(F32)).reshape(-1)
    pick = (dest.reshape(-1)[:, None] == jnp.arange(experts * capacity)[None, :]).astype(BF16)
    pick_scale = jnp.where(xl == 0, scale, 1.0)
    picked = jnp.dot(pick, parts, preferred_element_type=F32) * pick_scale[:, None]
    summed = (picked[:frames] + picked[frames:]).astype(BF16)
    mine = lax.all_to_all(
        jnp.broadcast_to(summed[None], (ranks,) + summed.shape), "y", 0, 0, tiled=True
    )

    mine, top, bottom = edge_rows(mine, out_grad[0], slope)
    halos = [rim for half in (0, 1) for rim in edge_rims(top, bottom, half)]
    other = lax.ppermute(mine, "xl", swap)
    block_out, resid_grad, glu_grad = backward_full(
        xl.reshape(1), mine, other, hidden_in, out_grad[0], slope, halos, dw_kernel, glu_in
    )

    hidden = weight_in.shape[1]
    w_in_grad = own_in + sum(piece[: width // 2].astype(F32) for piece in got)
    rest = [
        piece[width // 2 :].reshape(-1, hidden, hidden).transpose(1, 0, 2).reshape(hidden, -1)
        for piece in got
    ]
    w_out_grad = own_out + sum(piece.astype(F32) for piece in rest)
    return (
        block_out[None],
        resid_grad[None],
        glu_grad[None],
        w_in_grad[None],
        w_out_grad[None],
    )


def solution(mesh):
    size = mesh.shape["expert"]
    axes = {"tm": mesh.shape["tm"], "xl": 2, "y": size // 2, "dp": mesh.shape["dp"]}
    split = Mesh(mesh.devices.reshape(tuple(axes.values())), tuple(axes))
    expert = ("xl", "y")
    return jax.shard_map(
        shards,
        mesh=split,
        in_specs=(
            P("dp", "tm", None),
            P("dp", "tm", None),
            P(),
            P("tm", None, expert),
            P("tm", expert, None),
            P("dp", "tm", None),
            P("dp", "tm", None),
            P("dp", "tm"),
            P("dp", "tm", None),
        ),
        out_specs=(
            P("dp", "tm", None),
            P("dp", "tm", None),
            P("dp", "tm", None),
            P("tm", "dp", expert),
            P("tm", expert, "dp"),
        ),
        check_vma=False,
    )
```

```python
import functools

import jax
import jax.numpy as jnp
from jax import lax
from jax.experimental import pallas as pl
from jax.experimental.pallas import tpu as pltpu
from jax.sharding import Mesh, PartitionSpec as P

KERNEL = 31
HALF = KERNEL // 2
F32 = jnp.float32
BF16 = jnp.bfloat16
NT = (((1,), (1,)), ((), ()))
TN = (((0,), (0,)), ((), ()))


RIM = 16


def swish_slope(value):
    sig = jax.nn.sigmoid(value)
    return sig * (1.0 + value * (1.0 - sig))


def rims(top, bottom):
    size = lax.axis_size("tm")
    up = [(i, i + 1) for i in range(size - 1)]
    down = [(j, i) for i, j in up]
    return lax.ppermute(bottom, "tm", up), lax.ppermute(top, "tm", down)


def taps_sum(padded, taps, frames, start, step):
    total = None
    for residue in range(8):
        offsets = [(start + step * j, j) for j in range(KERNEL) if (start + step * j) % 8 == residue]
        reach = max(offset for offset, _ in offsets) - residue
        shifted = padded[residue : residue + reach + frames, :]
        for offset, j in offsets:
            base = offset - residue
            term = taps[j : j + 1, :] * shifted[base : base + frames]
            total = term if total is None else total + term
    return total


def glu(value, gate):
    return value.astype(F32) * jax.nn.sigmoid(gate.astype(F32))


def glu_conv(value, gate, before_value, before_gate, after_value, after_gate, taps, padded):
    frames = value.shape[0]
    padded[:RIM] = glu(before_value[...], before_gate[...])
    padded[RIM : RIM + frames] = glu(value[...], gate[...])
    padded[RIM + frames :] = glu(after_value[...], after_gate[...])
    return taps_sum(padded, taps, frames, RIM - HALF, 1)


def dispatch_kernel(
    experts,
    where_ref,
    value,
    gate,
    before_value,
    before_gate,
    after_value,
    after_gate,
    taps,
    resid,
    out_grad,
    ids,
    mix,
    kept,
    rows_ref,
    dest_ref,
    padded,
):
    frames = value.shape[0]
    total = rows_ref.shape[0]
    conv = glu_conv(value, gate, before_value, before_gate, after_value, after_gate, taps, padded)
    hidden_in = (resid[...].astype(F32) + conv * jax.nn.sigmoid(conv)).astype(BF16)
    first = where_ref[0] == 0
    chosen = jnp.where(first, hidden_in.astype(F32), out_grad[...].astype(F32)).astype(BF16)
    expert = lax.broadcasted_iota(jnp.int32, (experts, frames), 0)
    named = [jnp.where(ids[k : k + 1, :] == expert, 1.0, 0.0) for k in range(2)]
    earlier = lax.broadcasted_iota(jnp.int32, (frames, frames), 0) < lax.broadcasted_iota(
        jnp.int32, (frames, frames), 1
    )
    ahead = jnp.dot(
        (named[0] + named[1]).astype(BF16),
        jnp.where(earlier, 1.0, 0.0).astype(BF16),
        preferred_element_type=F32,
    )
    row = lax.broadcasted_iota(jnp.int32, (total, frames), 0)
    ones = jnp.zeros((total, frames), F32)
    factor = jnp.zeros((total, frames), F32)
    for k in range(2):
        slot = jnp.sum(named[k] * ahead, axis=0, keepdims=True).astype(jnp.int32)
        dest = ids[k : k + 1, :] * (total // experts) + slot
        dest_ref[k : k + 1, :] = dest
        hot = row == dest
        scale = mix[k : k + 1, :] * kept[...].astype(F32)
        ones = jnp.where(hot, 1.0, ones)
        factor = jnp.where(hot, scale, factor)
    ones = ones.astype(BF16)
    factor = jnp.sum(factor, axis=1, keepdims=True)
    rows = jnp.dot(ones, chosen, preferred_element_type=F32)
    rows_ref[...] = jnp.where(first, rows, rows * factor).astype(BF16)


def forward_kernel(
    value,
    gate,
    before_value,
    before_gate,
    after_value,
    after_gate,
    taps,
    resid,
    hidden_ref,
    slope_ref,
    padded,
):
    conv = glu_conv(value, gate, before_value, before_gate, after_value, after_gate, taps, padded)
    sig = jax.nn.sigmoid(conv)
    hidden_ref[...] = (resid[...].astype(F32) + conv * sig).astype(BF16)
    slope_ref[...] = sig * (1.0 + conv * (1.0 - sig))


def edges_kernel(part_ref, out_grad, slope, edges_ref):
    for at in range(part_ref.shape[0]):
        cols = slice(at * part_ref.shape[2], (at + 1) * part_ref.shape[2])
        hid_grad = out_grad[:, cols].astype(F32) + part_ref[at].astype(F32)
        edges_ref[:, cols] = (hid_grad * slope[:, cols]).astype(BF16)


def outputs_kernel(summed, hidden, out_grad, slope, block_ref, resid_ref, conv_grad_ref):
    blocks = summed.shape[0] // 2
    for at in range(blocks):
        cols = slice(at * summed.shape[2], (at + 1) * summed.shape[2])
        moe = summed[at].astype(F32)
        block_ref[:, cols] = (hidden[:, cols].astype(F32) + moe).astype(BF16)
        hid_grad = out_grad[:, cols].astype(F32) + summed[blocks + at].astype(F32)
        resid_ref[:, cols] = hid_grad.astype(BF16)
        conv_grad_ref[:, cols] = hid_grad * slope[:, cols]


def backward_kernel(conv_grad, before, after, taps, glu_in, out, padded):
    frames, width = conv_grad.shape
    cols = padded.shape[1]

    def step(index, carry):
        at = pl.ds(pl.multiple_of(index * cols, cols), cols)
        at_gate = pl.ds(pl.multiple_of(width + index * cols, cols), cols)
        padded[:RIM] = before[:, at].astype(F32)
        padded[RIM : RIM + frames] = conv_grad[:, at]
        padded[RIM + frames :] = after[:, at].astype(F32)
        back = taps_sum(padded, taps[:, at], frames, RIM + HALF, -1)
        sig = jax.nn.sigmoid(glu_in[:, at_gate].astype(F32))
        grad = back * sig
        out[:, at] = grad.astype(BF16)
        out[:, at_gate] = (grad * glu_in[:, at].astype(F32) * (1.0 - sig)).astype(BF16)
        return carry

    lax.fori_loop(0, width // cols, step, 0)


def gather_columns(rows_ref, hid, grad):
    parts = rows_ref.shape[0] // 2
    cols = rows_ref.shape[2]
    for part in range(parts):
        side, at = divmod(part, parts // 2)
        hid[side, :, at * cols : (at + 1) * cols] = rows_ref[part]
        grad[side, :, at * cols : (at + 1) * cols] = rows_ref[parts + part]


def expert_kernel(rows_ref, win_a, win_b, wout_a, wout_b, act_ref, act_grad_ref, out_ref, hid, grad):
    gather_columns(rows_ref, hid, grad)
    width = hid.shape[2]
    result = [0.0, 0.0]
    part = [0.0, 0.0]
    for which, (w_in, w_out) in enumerate(((win_a, wout_a), (win_b, wout_b))):
        pre = sum(
            jnp.dot(hid[s], w_in[s * width : (s + 1) * width, :], preferred_element_type=F32)
            for s in range(2)
        )
        back = sum(
            lax.dot_general(
                grad[s], w_out[:, s * width : (s + 1) * width], NT, preferred_element_type=F32
            )
            for s in range(2)
        )
        sig = jax.nn.sigmoid(pre)
        act = (pre * sig).astype(BF16)
        act_grad = (back * (sig * (1.0 + pre * (1.0 - sig)))).astype(BF16)
        act_ref[which] = act
        act_grad_ref[which] = act_grad
        for s in range(2):
            result[s] += jnp.dot(
                act, w_out[:, s * width : (s + 1) * width], preferred_element_type=F32
            )
            part[s] += lax.dot_general(
                act_grad, w_in[s * width : (s + 1) * width, :], NT, preferred_element_type=F32
            )
    blocks = out_ref.shape[0] // 2
    cols = out_ref.shape[2]
    for index in range(blocks):
        side, at = divmod(index, blocks // 2)
        out_ref[index] = result[side][:, at * cols : (at + 1) * cols].astype(BF16)
        out_ref[blocks + index] = part[side][:, at * cols : (at + 1) * cols].astype(BF16)


def grads_kernel(pieces, dp_ref, rows_ref, act_ref, act_grad_ref, *refs):
    *outs, hid, grad = refs
    gather_columns(rows_ref, hid, grad)
    mine = dp_ref[0]
    hidden = act_ref.shape[2]
    for which, other in pieces:
        side = mine if other == 0 else 1 - mine
        g_in = lax.dot_general(hid[side], act_grad_ref[which], TN, preferred_element_type=F32)
        g_out = lax.dot_general(act_ref[which], grad[side], TN, preferred_element_type=F32)
        if which == 0 and other == 0:
            own_in, own_out, *outs = outs
            own_in[...] = g_in
            own_out[...] = g_out
        else:
            width = g_in.shape[0]
            send, *outs = outs
            send[:width] = g_in.astype(BF16)
            for piece in range(g_out.shape[1] // hidden):
                send[width + piece * hidden : width + (piece + 1) * hidden] = g_out[
                    :, piece * hidden : (piece + 1) * hidden
                ].astype(BF16)


def vmem(count):
    return [pl.BlockSpec(memory_space=pltpu.VMEM)] * count


def expert_rows(rows, win, win_other, wout, wout_other):
    parts, count, cols = rows.shape
    width = parts * cols // 2
    hidden = win.shape[1]
    flops = 16 * count * width * hidden
    return pl.pallas_call(
        expert_kernel,
        out_shape=(
            jax.ShapeDtypeStruct((2, count, hidden), BF16),
            jax.ShapeDtypeStruct((2, count, hidden), BF16),
            jax.ShapeDtypeStruct((parts, count, cols), BF16),
        ),
        in_specs=vmem(5),
        out_specs=tuple(vmem(3)),
        scratch_shapes=[pltpu.VMEM((2, count, width // 2), BF16)] * 2,
        compiler_params=pltpu.CompilerParams(vmem_limit_bytes=40 * 2**20),
        cost_estimate=pl.CostEstimate(flops=flops, bytes_accessed=5 * 2**20, transcendentals=0),
    )(rows, win, win_other, wout, wout_other)


def weight_grads(pieces, dp, rows, act, act_grad):
    parts, count, cols = rows.shape
    width = parts * cols // 2
    hidden = act.shape[2]
    shapes = []
    for piece in pieces:
        if piece == (0, 0):
            shapes.append(jax.ShapeDtypeStruct((width // 2, hidden), F32))
            shapes.append(jax.ShapeDtypeStruct((hidden, width // 2), F32))
        else:
            shapes.append(jax.ShapeDtypeStruct((width, hidden), BF16))
    return pl.pallas_call(
        functools.partial(grads_kernel, pieces),
        out_shape=tuple(shapes),
        in_specs=[pl.BlockSpec(memory_space=pltpu.SMEM)] + vmem(3),
        out_specs=tuple(vmem(len(shapes))),
        scratch_shapes=[pltpu.VMEM((2, count, width // 2), BF16)] * 2,
        compiler_params=pltpu.CompilerParams(vmem_limit_bytes=40 * 2**20),
        cost_estimate=pl.CostEstimate(
            flops=2 * len(pieces) * count * width * hidden,
            bytes_accessed=4 * 2**20,
            transcendentals=0,
        ),
    )(dp, rows, act, act_grad)


def glu_specs(frames, cols, blocks, place):
    def spec(rows, shift):
        return pl.BlockSpec((rows, cols), lambda i, *ref: (0, shift + place(i, *ref)))

    return [spec(rows, shift) for rows in (frames, RIM, RIM) for shift in (0, blocks)]


def dispatch_rows(
    where, glu_in, before, after, taps, resid, out_grad, ids, mix, kept, experts, total, cols
):
    frames, width = resid.shape
    blocks = width // cols

    def place(i, ref):
        return ref[1]

    def spec(rows):
        return pl.BlockSpec((rows, cols), lambda i, ref: (0, place(i, ref)))

    def whole(rows, columns):
        return pl.BlockSpec((rows, columns), lambda i, ref: (0, 0))

    return pl.pallas_call(
        functools.partial(dispatch_kernel, experts),
        out_shape=(
            jax.ShapeDtypeStruct((total, cols), BF16),
            jax.ShapeDtypeStruct((2, frames), jnp.int32),
        ),
        grid_spec=pltpu.PrefetchScalarGridSpec(
            num_scalar_prefetch=1,
            grid=(1,),
            in_specs=glu_specs(frames, cols, blocks, place)
            + [spec(KERNEL), spec(frames), spec(frames)]
            + [whole(2, frames), whole(2, frames), whole(1, frames)],
            out_specs=(whole(total, cols), whole(2, frames)),
            scratch_shapes=[pltpu.VMEM((frames + 2 * RIM, cols), F32)],
        ),
        compiler_params=pltpu.CompilerParams(vmem_limit_bytes=56 * 2**20),
        cost_estimate=pl.CostEstimate(flops=2 * 10**7, bytes_accessed=2**20, transcendentals=0),
    )(where, glu_in, glu_in, before, before, after, after, taps, resid, out_grad, ids, mix, kept)


def column(rows, cols):
    return pl.BlockSpec((rows, cols), lambda i: (0, i))


def forward_full(glu_in, before, after, taps, resid, cols):
    frames, width = resid.shape
    blocks = width // cols
    return pl.pallas_call(
        forward_kernel,
        grid=(blocks,),
        out_shape=(
            jax.ShapeDtypeStruct((frames, width), BF16),
            jax.ShapeDtypeStruct((frames, width), F32),
        ),
        in_specs=glu_specs(frames, cols, blocks, lambda i: i)
        + [column(KERNEL, cols), column(frames, cols)],
        out_specs=(column(frames, cols), column(frames, cols)),
        scratch_shapes=[pltpu.VMEM((frames + 2 * RIM, cols), F32)],
        compiler_params=pltpu.CompilerParams(vmem_limit_bytes=16 * 2**20),
        cost_estimate=pl.CostEstimate(flops=2 * 10**7, bytes_accessed=2**21, transcendentals=0),
    )(glu_in, glu_in, before, before, after, after, taps, resid)


def edge_rows(summed, out_grad, slope):
    blocks, frames, cols = summed.shape
    blocks //= 2
    width = blocks * cols
    last = frames // RIM - 1
    row = pl.BlockSpec((RIM, width), lambda i: (i * last, 0))
    return pl.pallas_call(
        edges_kernel,
        grid=(2,),
        out_shape=jax.ShapeDtypeStruct((2 * RIM, width), BF16),
        in_specs=[pl.BlockSpec((blocks, RIM, cols), lambda i: (1, i * last, 0)), row, row],
        out_specs=pl.BlockSpec((RIM, width), lambda i: (i, 0)),
        compiler_params=pltpu.CompilerParams(vmem_limit_bytes=16 * 2**20),
        cost_estimate=pl.CostEstimate(flops=10**5, bytes_accessed=2**18, transcendentals=0),
    )(summed, out_grad, slope)


def finish(summed, hidden_in, out_grad, slope):
    half = jax.ShapeDtypeStruct(hidden_in.shape, BF16)
    return pl.pallas_call(
        outputs_kernel,
        out_shape=(half, half, jax.ShapeDtypeStruct(hidden_in.shape, F32)),
        in_specs=vmem(4),
        out_specs=tuple(vmem(3)),
        compiler_params=pltpu.CompilerParams(vmem_limit_bytes=16 * 2**20),
        cost_estimate=pl.CostEstimate(flops=10**6, bytes_accessed=2**21, transcendentals=0),
    )(summed, hidden_in, out_grad, slope)


def backward_full(conv_grad, before, after, taps, glu_in, cols):
    frames = conv_grad.shape[0]
    return pl.pallas_call(
        backward_kernel,
        out_shape=jax.ShapeDtypeStruct(glu_in.shape, BF16),
        in_specs=vmem(5),
        out_specs=pl.BlockSpec(memory_space=pltpu.VMEM),
        scratch_shapes=[pltpu.VMEM((frames + 2 * RIM, cols), F32)],
        compiler_params=pltpu.CompilerParams(vmem_limit_bytes=16 * 2**20),
        cost_estimate=pl.CostEstimate(flops=2 * 10**7, bytes_accessed=2**21, transcendentals=0),
    )(conv_grad, before, after, taps, glu_in)


def shards(resid, glu_input, dw_kernel, w_in, w_out, expert_ids, mix_weights, frame_kept, out_grad):
    frames = resid.shape[1]
    width = resid.shape[2]
    experts = lax.axis_size("tm")
    ranks = lax.axis_size("y")
    capacity = 4 * frames // experts
    half_cap = capacity // 2
    cols = width // ranks
    xl = lax.axis_index("xl")
    y = lax.axis_index("y")
    dp = lax.axis_index("dp")
    weight_in = w_in[0]
    weight_out = w_out[0]
    swap = [(0, 1), (1, 0)]
    swap_both = [(0, 3), (3, 0), (1, 2), (2, 1)]

    glu_in = glu_input[0]
    before, after = rims(glu_in[:RIM], glu_in[frames - RIM :])

    ids = expert_ids[0].T
    mix = mix_weights[0].T
    rows, dest = dispatch_rows(
        jnp.stack([xl, y]),
        glu_in,
        before,
        after,
        dw_kernel,
        resid[0],
        out_grad[0],
        ids,
        mix,
        frame_kept,
        experts,
        experts * capacity,
        cols,
    )
    rows = lax.all_to_all(rows.reshape(experts, capacity, cols), "tm", 0, 0, tiled=True)
    hidden_in, slope = forward_full(glu_in, before, after, dw_kernel, resid[0], cols)
    win_other = lax.ppermute(weight_in, "xl", swap)
    wout_other = lax.ppermute(weight_out, ("xl", "dp"), swap_both)
    rows = rows.reshape(experts, 2, half_cap, cols).transpose(1, 0, 2, 3)
    rows = rows.reshape(2, 1, experts * half_cap, cols)
    rows = jnp.broadcast_to(rows, (2, ranks) + rows.shape[2:]).reshape((-1,) + rows.shape[2:])
    rows = lax.all_to_all(rows, ("xl", "y"), 0, 0, tiled=True)

    act, act_grad, parts = expert_rows(rows, weight_in, win_other, weight_out, wout_other)
    parts = lax.all_to_all(parts, ("xl", "y"), 0, 0, tiled=True)
    pieces = [(0, 0), (0, 1), (1, 0), (1, 1)]
    own_in, own_out, *send = weight_grads(pieces, dp.reshape(1), rows, act, act_grad)
    got_both = lax.ppermute(send[2], ("xl", "dp"), swap_both)
    got_both, send_dp, send_xl = lax.optimization_barrier((got_both, send[0], send[1]))
    got_dp = lax.ppermute(send_dp, "dp", swap)
    got_xl = lax.ppermute(send_xl, "xl", swap)
    parts, got_both = lax.optimization_barrier((parts, got_both))

    parts = parts.reshape(2, ranks, experts, half_cap, cols).astype(F32).sum(axis=1)
    parts = parts.astype(BF16).transpose(1, 0, 2, 3).reshape(experts, capacity, cols)
    parts = lax.all_to_all(parts, "tm", 0, 0, tiled=True).reshape(experts * capacity, cols)
    parts, got_dp, got_xl = lax.optimization_barrier((parts, got_dp, got_xl))
    got = (got_dp, got_xl, got_both)
    scale = (mix * frame_kept.astype(F32)).reshape(-1)
    pick = (dest.reshape(-1)[:, None] == jnp.arange(experts * capacity)[None, :]).astype(BF16)
    pick_scale = jnp.where(xl == 0, scale, 1.0)
    picked = jnp.dot(pick, parts, preferred_element_type=F32) * pick_scale[:, None]
    summed = (picked[:frames] + picked[frames:]).astype(BF16)
    summed = lax.all_to_all(
        jnp.broadcast_to(summed[None], (2 * ranks,) + summed.shape), ("xl", "y"), 0, 0, tiled=True
    )

    edges = edge_rows(summed, out_grad[0], slope)
    before, after = rims(edges[:RIM], edges[RIM:])
    block_out, resid_grad, conv_grad = finish(summed, hidden_in, out_grad[0], slope)
    glu_grad = backward_full(conv_grad, before, after, dw_kernel, glu_in, cols)

    hidden = weight_in.shape[1]
    w_in_grad = own_in + sum(piece[: width // 2].astype(F32) for piece in got)
    rest = [
        piece[width // 2 :].reshape(-1, hidden, hidden).transpose(1, 0, 2).reshape(hidden, -1)
        for piece in got
    ]
    w_out_grad = own_out + sum(piece.astype(F32) for piece in rest)
    return (
        block_out[None],
        resid_grad[None],
        glu_grad[None],
        w_in_grad[None],
        w_out_grad[None],
    )


def solution(mesh):
    size = mesh.shape["expert"]
    axes = {"tm": mesh.shape["tm"], "xl": 2, "y": size // 2, "dp": mesh.shape["dp"]}
    split = Mesh(mesh.devices.reshape(tuple(axes.values())), tuple(axes))
    expert = ("xl", "y")
    return jax.shard_map(
        shards,
        mesh=split,
        in_specs=(
            P("dp", "tm", None),
            P("dp", "tm", None),
            P(),
            P("tm", None, expert),
            P("tm", expert, None),
            P("dp", "tm", None),
            P("dp", "tm", None),
            P("dp", "tm"),
            P("dp", "tm", None),
        ),
        out_specs=(
            P("dp", "tm", None),
            P("dp", "tm", None),
            P("dp", "tm", None),
            P("tm", "dp", expert),
            P("tm", expert, "dp"),
        ),
        check_vma=False,
    )
```
